128 devices in a mesh: mc: 8 (over z, core), space: 16 (over x, y).
Axes of the slice: x: 4, y: 4, z: 4, core: 2. Of those that a mesh axis runs over, the one named last changes fastest.
Arguments:
- orbit_state: float32 [6, 4194304], P(None, ('mc', 'space')), parts along dimension 1, may hold values from -1.3 to 1.3, as said below
- object_props: float32 [3, 4194304], P(None, ('mc', 'space')), parts along dimension 1, may hold values from 0.5 to 2
- density_table: float32 [64], replicated, may hold values from -1 to 1
- block_cube: int32 [32768], P(('mc', 'space')), parts along dimension 0, may hold values from 0 to 2047, as said below
Outputs:
- next_state: float32 [6, 4194304], P(None, ('mc', 'space')), parts along dimension 1
- collision_rate: float32 [4194304], P(('mc', 'space')), parts along dimension 0
The draws below stay inside these ranges and needn't reach their ends.
There are 8 independent parts, one for each index of `mc`. The reference program is written for one: setup_inputs(seed, part) draws one part's arguments, and reference() takes and returns one part's arrays. A program takes and returns all parts, laid end to end along the dimension named above; an argument that names none is the same for every part. Nothing has to cross between parts.
Inputs may be any that keep to these rules, and one draw needn't show every extreme that they name: `orbit_state`: rows 0 to 2 are a position with 1.08 <= |r| <= 1.3, rows 3 to 5 a velocity of speed between 0.86 and 0.98. `block_cube`: cube c is owned by the device of index c // 128 along space. No cube holds more than 4 blocks in all, and in every draw some cube holds exactly 4. The blocks of one device include at most 32 whose cubes have any one owner, and in every draw some owner receives exactly 32 blocks from every device.
All inputs are finite; a program needn't handle non-finite values.
Results may differ from the reference program's by a relative error of at most 0.0003.
Values sent between devices are 32-bit elements; how exact they have to be, the bound alone decides.
A program may use at most 64 MiB of HBM per device.

```python
import math
import jax
import jax.numpy as jnp
from jax import lax

BLK = 128
BLK_DEV = 256
MOST = 4
SUB = 16
NTAB = 64
CAP = 32
CUBE_DEV = 128
NBLOCKS = 4096
OBJECTS = 524288
N_SPACE = 16


def draw_orbit_state(key, part):
    key_alt, key_dir, key_tan, key_speed, key_radial = jax.random.split(jax.random.fold_in(key, 11), 5)
    height = jax.random.uniform(key_alt, (OBJECTS,), jnp.float32, 0.08, 0.3)
    normal_dir = jax.random.normal(key_dir, (3, OBJECTS), jnp.float32)
    unit_dir = normal_dir / jnp.sqrt(jnp.sum(normal_dir * normal_dir, axis=0) + 1e-12)
    tangent = jax.random.normal(key_tan, (3, OBJECTS), jnp.float32)
    tangent = tangent - jnp.sum(tangent * unit_dir, axis=0) * unit_dir
    tangent = tangent / jnp.sqrt(jnp.sum(tangent * tangent, axis=0) + 1e-12)
    radius = 1.0 + height
    circular = jax.random.uniform(key_speed, (OBJECTS,), jnp.float32, 0.99, 1.01) / jnp.sqrt(radius)
    radial = 0.01 * jnp.clip(jax.random.normal(key_radial, (OBJECTS,), jnp.float32), -3.0, 3.0)
    position = radius * unit_dir
    velocity = circular * (tangent + radial * unit_dir)
    return jnp.concatenate([position, velocity], axis=0)


def draw_block_cube(key, part):
    base_key = jax.random.fold_in(key, 29)
    key_hot, key_pick, key_order, key_slot = jax.random.split(base_key, 4)
    hot_owner = jax.random.randint(key_hot, (), 0, N_SPACE)
    other_width = (N_SPACE - 1) * CAP
    others = jnp.arange(other_width) // CAP
    others = others + (others >= hot_owner).astype(jnp.int32)
    pick_score = jax.random.randint(key_pick, (N_SPACE, other_width), 0, 1 << 16) * other_width + jnp.arange(other_width)[None, :]
    picked = others[jnp.argsort(pick_score, axis=1)[:, :BLK_DEV - CAP]]
    owners = jnp.concatenate([jnp.full((N_SPACE, CAP), hot_owner, jnp.int32), picked.astype(jnp.int32)], axis=1)
    order_score = jax.random.randint(key_order, (N_SPACE, BLK_DEV), 0, 1 << 16) * BLK_DEV + jnp.arange(BLK_DEV)[None, :]
    owners = jnp.take_along_axis(owners, jnp.argsort(order_score, axis=1), axis=1).reshape(NBLOCKS)
    onehot = (owners[:, None] == jnp.arange(N_SPACE)[None, :]).astype(jnp.int32)
    owner_rank = jnp.sum((jnp.cumsum(onehot, axis=0) - onehot) * onehot, axis=1)
    slot_total = CUBE_DEV * MOST
    slot_score = jax.random.randint(key_slot, (N_SPACE, slot_total), 0, 1 << 16) * slot_total + jnp.arange(slot_total)[None, :]
    slot_perm = jnp.argsort(slot_score, axis=1)
    local_cube = slot_perm[owners, owner_rank] // MOST
    return (owners * CUBE_DEV + local_cube).astype(jnp.int32)


def steps_of(key, shape, cuts, least, high):
    factor_of = 1.0
    for dim, shards_of in cuts:
        steps = jax.random.uniform(jax.random.fold_in(jax.random.fold_in(key, 6), dim), (shards_of,), jnp.float32, least / len(cuts), high / len(cuts))
        factor_of = factor_of * jnp.repeat(jnp.exp(steps), shape[dim] // shards_of).reshape((-1,) + (1,) * (len(shape) - 1 - dim))
    return factor_of


def setup_inputs(seed: int = 0, part: int = 0) -> dict:
    key_list = jax.random.split(jax.random.key(seed), 5)
    part_keys = jax.random.split(jax.random.fold_in(key_list[4], part), 5)
    return {
        "orbit_state": draw_orbit_state(jax.random.fold_in(jax.random.fold_in(key_list[4], part), 71), part),
        "object_props": jnp.clip(jnp.exp(math.log(2.0) - 1.3862944 * jax.random.uniform(part_keys[1], (3, OBJECTS), jnp.float32) ** steps_of(part_keys[1], (3, OBJECTS), ((1, 16),), -0.2, 0.2)), 0.5, 2.0),
        "density_table": jnp.clip(jax.random.uniform(key_list[2], (NTAB,), jnp.float32, -1.0, 1.0), -1.0, 1.0),
        "block_cube": draw_block_cube(jax.random.fold_in(jax.random.fold_in(key_list[4], part), 71), part),
    }


TIME_STEP = 0.2
EARTH_SPIN = 0.0588
J2_COEF = 0.00108263
DRAG_SCALE = 0.008
SCALE_HEIGHT = 0.1
TABLE_TOP = 0.4
SPEED_FLOOR = 0.04

def propagate(orbit_part, prop_part, density_table):
    position = orbit_part[0:3]
    velocity = orbit_part[3:6]
    ballistic = prop_part[2]
    alt_grid = jnp.arange(NTAB).astype(density_table.dtype)
    for substep in range(SUB):
        radius_sq = lax.optimization_barrier(jnp.sum(position * position, axis=0))
        radius = jnp.sqrt(radius_sq)
        height = radius - 1.0
        table_coord = height * ((NTAB - 1) / TABLE_TOP)
        hat_weights = jnp.maximum(0.0, 1.0 - jnp.abs(table_coord[None, :] - alt_grid[:, None]))
        log_density = jnp.dot(density_table[None, :], hat_weights, precision=lax.Precision.HIGHEST)[0] - height / SCALE_HEIGHT
        density = DRAG_SCALE * jnp.exp(log_density)
        relative = jnp.stack([velocity[0] + EARTH_SPIN * position[1], velocity[1] - EARTH_SPIN * position[0], velocity[2]])
        air_speed = jnp.sqrt(lax.optimization_barrier(jnp.sum(relative * relative, axis=0)))
        inv_cube = 1.0 / (radius_sq * radius)
        polar_ratio = position[2] * position[2] / radius_sq
        oblate_factor = 1.5 * J2_COEF / (radius_sq * radius_sq * radius)
        shape_term = jnp.stack([1.0 - 5.0 * polar_ratio, 1.0 - 5.0 * polar_ratio, 3.0 - 5.0 * polar_ratio])
        acceleration = -position * inv_cube - oblate_factor * position * shape_term - density * ballistic * air_speed * relative
        velocity = velocity + TIME_STEP * acceleration
        position = position + TIME_STEP * velocity
    return jnp.concatenate([position, velocity], axis=0)

def propagate_all(orbit_state, object_props, density_table):
    total_count = orbit_state.shape[1]
    span_width = math.gcd(total_count, 4096)
    groups = total_count // span_width
    stacked = orbit_state.reshape(6, groups, span_width).transpose(1, 0, 2)
    prop_stack = object_props.reshape(3, groups, span_width).transpose(1, 0, 2)
    advanced = lax.map(lambda packed: propagate(packed[0], packed[1], density_table), (stacked, prop_stack))
    return advanced.transpose(1, 0, 2).reshape(6, total_count)

def group_rates(group_ids, partners, partner_ok, velocity, radius, weight):
    group_size = group_ids.shape[0]
    own_vel = velocity[:, group_ids]
    peer_vel = velocity[:, partners].reshape(3, group_size, MOST * BLK)
    diff_sq = jnp.zeros((group_size, BLK, MOST * BLK), velocity.dtype)
    for component in range(3):
        gap = own_vel[component][:, :, None] - peer_vel[component][:, None, :]
        diff_sq = diff_sq + gap * gap
    own_rad = radius[group_ids][:, :, None]
    peer_rad = radius[partners].reshape(group_size, 1, MOST * BLK)
    peer_wt = weight[partners].reshape(group_size, 1, MOST * BLK)
    same_block = jnp.repeat(partners == group_ids[:, None], BLK, axis=1)[:, None, :]
    column_ok = jnp.repeat(partner_ok, BLK, axis=1)[:, None, :]
    same_index = (jnp.arange(BLK)[:, None] == (jnp.arange(MOST * BLK) % BLK)[None, :])[None, :, :]
    keep_mask = column_ok & jnp.logical_not(same_block & same_index)
    pair_term = jnp.where(keep_mask, peer_wt * (own_rad + peer_rad) ** 2 * jnp.sqrt(diff_sq + SPEED_FLOOR), 0.0)
    return weight[group_ids] * lax.optimization_barrier(jnp.sum(pair_term, axis=2)) / (MOST * BLK)

def reference(orbit_state, object_props, density_table, block_cube):
    next_state = propagate_all(orbit_state, object_props, density_table)
    velocity = next_state[3:6].reshape(3, NBLOCKS, BLK)
    radius = object_props[0].reshape(NBLOCKS, BLK)
    weight = object_props[1].reshape(NBLOCKS, BLK)
    block_index = jnp.arange(NBLOCKS).astype(jnp.int32)

    def one_group(first_block):
        group_ids = (first_block + jnp.arange(16)).astype(jnp.int32)
        same_cube = block_cube[group_ids][:, None] == block_cube[None, :]
        scores = jnp.where(same_cube, 2 * NBLOCKS - block_index[None, :], NBLOCKS - block_index[None, :]).astype(jnp.int32)
        values, partners = lax.top_k(scores, MOST)
        return group_rates(group_ids, partners.astype(jnp.int32), values > NBLOCKS, velocity, radius, weight)
    block_rates = lax.map(one_group, jnp.arange(0, NBLOCKS, 16).astype(jnp.int32))
    return (next_state, block_rates.reshape(OBJECTS))
```

```python
import functools

import jax
import jax.numpy as jnp
from jax import lax
from jax.experimental import pallas as pl
from jax.experimental.pallas import tpu as pltpu
from jax.sharding import PartitionSpec as P

F32 = jnp.float32
BF16 = jnp.bfloat16
BLK = 128
NB = 256
NS = 16
CAP = 32
SLOTS = NS * CAP
CUBES = 128
MOST = 4
SUB = 16
ROWS = 5 * CAP + 8
KF = 32
PITCH = SLOTS + 8

TIME_STEP = 0.2
EARTH_SPIN = 0.0588
J2_COEF = 0.00108263
DRAG_SCALE = 0.008
TABLE_SCALE = 63 / 0.4
SPEED_FLOOR = 0.04


def iota(shape, dim):
    return lax.broadcasted_iota(jnp.int32, shape, dim)


def split2(x):
    high = x.astype(BF16)
    return high, (x - high.astype(F32)).astype(BF16)


def columns_of(row):
    parts = [
        jnp.transpose(jnp.broadcast_to(row[:, k : k + BLK], (BLK, BLK)))
        for k in range(0, row.shape[1], BLK)
    ]
    return jnp.concatenate(parts, axis=0)


def rank_row(row):
    n = row.shape[1]
    column = columns_of(row)
    ranks = []
    for k in range(0, n, BLK):
        earlier = iota((n, BLK), 0) < iota((n, BLK), 1) + k
        same = column == row[:, k : k + BLK]
        ranks.append(jnp.sum(jnp.where(earlier & same, 1.0, 0.0), axis=0, keepdims=True))
    return jnp.concatenate(ranks, axis=1)


def block_slots(cube_row):
    owner = lax.shift_right_logical(cube_row, 7).astype(F32)
    return owner * CAP + rank_row(owner)


def substep(x, y, z, vx, vy, vz, drag, tab, slope):
    r2 = x * x + y * y + z * z
    ri = lax.rsqrt(r2)
    h = r2 * ri - 1.0
    coord = jnp.clip(h * TABLE_SCALE, -1.0, 64.0)
    below = jnp.floor(coord)
    frac = coord - below
    index = below.astype(jnp.int32) + 1
    base = jnp.concatenate(
        [jnp.take_along_axis(tab, index[k : k + 8], axis=1) for k in range(0, x.shape[0], 8)], axis=0
    )
    rise = jnp.concatenate(
        [jnp.take_along_axis(slope, index[k : k + 8], axis=1) for k in range(0, x.shape[0], 8)], axis=0
    )
    density = jnp.exp(base + frac * rise - h * 10.0)
    ux = vx + EARTH_SPIN * y
    uy = vy - EARTH_SPIN * x
    u2 = ux * ux + uy * uy + vz * vz
    speed = u2 * lax.rsqrt(jnp.maximum(u2, 1e-36))
    pull = density * drag * speed
    i2 = ri * ri
    i3 = i2 * ri
    oblate = (1.5 * J2_COEF * TIME_STEP) * (i2 * i3)
    near = TIME_STEP * i3 + oblate * (1.0 - 5.0 * (z * z * i2))
    vx = vx - x * near - pull * ux
    vy = vy - y * near - pull * uy
    vz = vz - z * (near + 2.0 * oblate) - pull * vz
    return x + TIME_STEP * vx, y + TIME_STEP * vy, z + TIME_STEP * vz, vx, vy, vz


def propagate_kernel(chunk, orbit, props, table, cube, next_out, send, rows, prows, state, planes):
    def spread(b, carry):
        col = pl.ds(pl.multiple_of(b * BLK, BLK), BLK)
        at = pl.multiple_of(b * 8, 8)
        rows[pl.ds(at, 6), :] = orbit[:, col]
        prows[pl.ds(at, 3), :] = props[:, col]
        return carry

    lax.fori_loop(0, NB, spread, 0, unroll=8)

    tab = jnp.concatenate([table[...], jnp.zeros((1, 64), F32)], axis=1)
    tab = pltpu.roll(jnp.broadcast_to(tab, (8, BLK)), 1, 1)
    slope = pltpu.roll(tab, BLK - 1, 1) - tab

    def advance(g, carry):
        def load(ref, c):
            return jnp.concatenate(
                [
                    ref[pl.ds(g * (chunk * 8) + k * 8 + c, 8, stride=8), :]
                    for k in range(0, chunk, 8)
                ],
                axis=0,
            )

        at = pl.ds(pl.multiple_of(g * chunk, chunk), chunk)
        now = tuple(load(rows, c) for c in range(6))
        drag = load(prows, 2) * (DRAG_SCALE * TIME_STEP)
        planes[3, at, :] = load(prows, 0)
        planes[4, at, :] = load(prows, 1)
        now = lax.fori_loop(0, SUB, lambda s, v: substep(*v, drag, tab, slope), now, unroll=2)
        for c in range(6):
            for k in range(0, chunk, 8):
                rows[pl.ds(g * (chunk * 8) + k * 8 + c, 8, stride=8), :] = now[c][k : k + 8]
        for c in range(3):
            planes[c, at, :] = now[3 + c]
        return carry

    lax.fori_loop(0, NB // chunk, advance, 0)

    def collect(b, carry):
        col = pl.ds(pl.multiple_of(b * BLK, BLK), BLK)
        next_out[:, col] = rows[pl.ds(pl.multiple_of(b * 8, 8), 6), :]
        return carry

    lax.fori_loop(0, NB, collect, 0, unroll=8)

    slot = block_slots(cube[...])
    pick = jnp.where(slot == iota((SLOTS, NB), 0).astype(F32), 1.0, 0.0).astype(BF16)
    for c in range(5):
        high, low = split2(planes[c])
        got = jnp.dot(pick, jnp.concatenate([high, low], axis=1), preferred_element_type=F32)
        send[:, c * CAP : (c + 1) * CAP, :] = (got[:, :BLK] + got[:, BLK:]).reshape(NS, CAP, BLK)
    local = ((cube[...] & (CUBES - 1)) + 1).astype(F32)
    ids = jnp.dot(pick, columns_of(local).astype(BF16), preferred_element_type=F32)
    id_rows = []
    for q in range(SLOTS // BLK):
        line = jnp.transpose(ids[q * BLK : (q + 1) * BLK])[0:1]
        id_rows.append(jnp.broadcast_to(line, (4, BLK)))
    id_rows = jnp.concatenate(id_rows, axis=0)
    mine = lax.shift_right_logical(iota((NS, BLK), 1), 5) == (iota((NS, BLK), 0) & 3)
    id_rows = jnp.where(mine, id_rows, 0.0)
    id_rows = id_rows + pltpu.roll(id_rows, 64, 1)
    id_rows = id_rows + pltpu.roll(id_rows, 32, 1)
    send[:, 5 * CAP :, :] = jnp.broadcast_to(id_rows[:, None, :], (NS, 8, BLK))


def features(planes):
    v, (rh, rm), (wh, wm) = planes[:3], planes[3], planes[4]
    radius, weight = rh + rm, wh + wm
    full = [h + m for h, m in v]
    norm = full[0] * full[0] + full[1] * full[1] + full[2] * full[2]

    def thirds(x):
        a = x.astype(BF16).astype(F32)
        b = (x - a).astype(BF16).astype(F32)
        return [a, b, x - a - b]

    one = jnp.ones_like(radius)
    left, right = [], []
    for h, m in v:
        left += [h, h, m, m]
        right += [-2.0 * h, -2.0 * m, -2.0 * h, -2.0 * m]
    left += thirds(norm) + [one, one, one]
    right += [one, one, one] + thirds(norm + SPEED_FLOOR)
    p, q, t = weight, weight * radius, weight * radius * radius

    def halves(x):
        a = x.astype(BF16).astype(F32)
        return a, x - a

    (ph, pm), (qh, qm), (th, tm) = halves(p), halves(q), halves(t)
    left += [th, th, tm, 2.0 * qh, 2.0 * qh, 2.0 * qm, ph, ph, pm]
    right += [ph, pm, ph, qh, qm, qh, th, tm, th]
    return left, right


def pair_kernel(recv, back, left, right, rate):
    got = recv[:, 5 * CAP, :]
    mine = lax.shift_right_logical(iota((NS, BLK), 1), 5) == (iota((NS, BLK), 0) & 3)
    got = jnp.where(mine, got, 0.0)
    ids = jnp.concatenate(
        [jnp.sum(got[4 * q : 4 * q + 4], axis=0, keepdims=True) for q in range(4)], axis=1
    )
    place = jnp.where(ids > 0.0, (ids - 1.0) * MOST + rank_row(ids), -1.0)
    pick = jnp.where(place == iota((SLOTS, SLOTS), 0).astype(F32), 1.0, 0.0).astype(BF16)
    planes = []
    for c in range(5):
        plane = recv[:, c * CAP : (c + 1) * CAP, :].reshape(SLOTS, BLK)
        high, low = split2(plane)
        out = jnp.dot(pick, jnp.concatenate([high, low], axis=1), preferred_element_type=F32)
        planes.append((out[:, :BLK], out[:, BLK:]))
    lefts, rights = features(planes)
    zero = jnp.zeros((SLOTS, BLK), F32)
    for f in range(KF):
        left[f * PITCH : f * PITCH + SLOTS, :] = lefts[f] if f < len(lefts) else zero
        right[f * PITCH : f * PITCH + SLOTS, :] = rights[f] if f < len(rights) else zero

    gap_rows = iota((KF, BLK), 0) < 18
    off_diag = iota((BLK, BLK), 0) != iota((BLK, BLK), 1)

    def one_cube(q):
        base = q * MOST
        lhs = jnp.concatenate(
            [left[pl.ds(base + m, KF, stride=PITCH), :].astype(BF16) for m in range(MOST)], axis=1
        )
        row_sums = [None] * MOST
        out = []
        for c in range(MOST):
            r = right[pl.ds(base + c, KF, stride=PITCH), :]
            rhs = jnp.concatenate(
                [jnp.where(gap_rows, r, 0.0), jnp.where(gap_rows, 0.0, r)], axis=1
            ).astype(BF16)
            tiles = lax.dot_general(
                lhs[:, : (c + 1) * BLK], rhs, (((0,), (0,)), ((), ())), preferred_element_type=F32
            )
            total = None
            for a in range(c + 1):
                gap = jnp.maximum(tiles[a * BLK : (a + 1) * BLK, :BLK], SPEED_FLOOR)
                pair = tiles[a * BLK : (a + 1) * BLK, BLK:] * (gap * lax.rsqrt(gap))
                if a == c:
                    pair = jnp.where(off_diag, pair, 0.0)
                else:
                    row_sums[a] = pair if row_sums[a] is None else row_sums[a] + pair
                part = jnp.sum(pair.reshape(16, 8, BLK), axis=0)
                total = part if total is None else total + part
            out.append(total)
        for c in range(MOST):
            total = out[c]
            if row_sums[c] is not None:
                total = total + jnp.sum(jnp.transpose(row_sums[c]).reshape(16, 8, BLK), axis=0)
            rate[pl.ds(base + c, 1), :] = jnp.sum(total, axis=0, keepdims=True) * (1.0 / (MOST * BLK))

    def cubes(q, carry):
        one_cube(q)
        return carry

    lax.fori_loop(0, CUBES, cubes, 0)

    place_col = columns_of(place)
    unpick = jnp.concatenate(
        [
            jnp.where(place_col == (iota((SLOTS, BLK), 1) + k).astype(F32), 1.0, 0.0)
            for k in range(0, SLOTS, BLK)
        ],
        axis=1,
    ).astype(BF16)
    high, low = split2(rate[...])
    out = jnp.dot(unpick, jnp.concatenate([high, low], axis=1), preferred_element_type=F32)
    back[...] = (out[:, :BLK] + out[:, BLK:]).reshape(NS, CAP, BLK)


def unpack_kernel(back, cube, out):
    slot_col = columns_of(block_slots(cube[...]))
    pick = jnp.concatenate(
        [
            jnp.where(slot_col == (iota((NB, BLK), 1) + k).astype(F32), 1.0, 0.0)
            for k in range(0, SLOTS, BLK)
        ],
        axis=1,
    ).astype(BF16)
    high, low = split2(back[...].reshape(SLOTS, BLK))
    got = jnp.dot(pick, jnp.concatenate([high, low], axis=1), preferred_element_type=F32)
    out[...] = got[:, :BLK] + got[:, BLK:]


VMEM = pl.BlockSpec(memory_space=pltpu.VMEM)
PARAMS = pltpu.CompilerParams(vmem_limit_bytes=56 * 2**20)


def propagate_call(orbit_state, object_props, table, cube, chunk=32):
    return pl.pallas_call(
        functools.partial(propagate_kernel, chunk),
        out_shape=(
            jax.ShapeDtypeStruct((6, NB * BLK), F32),
            jax.ShapeDtypeStruct((NS, ROWS, BLK), F32),
        ),
        in_specs=[VMEM] * 4,
        out_specs=(VMEM, VMEM),
        scratch_shapes=[
            pltpu.VMEM((NB * 8, BLK), F32),
            pltpu.VMEM((NB * 8, BLK), F32),
            pltpu.VMEM((8, BLK), F32),
            pltpu.VMEM((5, NB, BLK), F32),
        ],
        compiler_params=PARAMS,
        name="propagate",
    )(orbit_state, object_props, table, cube)


def pair_call(recv):
    return pl.pallas_call(
        pair_kernel,
        out_shape=jax.ShapeDtypeStruct((NS, CAP, BLK), F32),
        in_specs=[VMEM],
        out_specs=VMEM,
        scratch_shapes=[
            pltpu.VMEM((KF * PITCH, BLK), F32),
            pltpu.VMEM((KF * PITCH, BLK), F32),
            pltpu.VMEM((SLOTS, BLK), F32),
        ],
        compiler_params=PARAMS,
        name="pairs",
    )(recv)


def unpack_call(back, cube):
    return pl.pallas_call(
        unpack_kernel,
        out_shape=jax.ShapeDtypeStruct((NB, BLK), F32),
        in_specs=[VMEM] * 2,
        out_specs=VMEM,
        compiler_params=PARAMS,
        name="unpack",
    )(back, cube)


def on_device(orbit_state, object_props, density_table, block_cube):
    cube = block_cube.reshape(1, NB)
    next_state, send = propagate_call(orbit_state, object_props, density_table.reshape(1, 64), cube)
    recv = lax.all_to_all(send, "space", split_axis=0, concat_axis=0, tiled=True)
    back = pair_call(recv)
    home = lax.all_to_all(back, "space", split_axis=0, concat_axis=0, tiled=True)
    return next_state, unpack_call(home, cube).reshape(NB * BLK)


def solution(mesh):
    placed = (P(None, ("mc", "space")), P(None, ("mc", "space")), P(), P(("mc", "space")))
    return jax.shard_map(
        on_device,
        mesh=mesh,
        in_specs=placed,
        out_specs=(P(None, ("mc", "space")), P(("mc", "space"))),
        check_vma=False,
    )
```

```python
import functools

import jax
import jax.numpy as jnp
from jax import lax
from jax.experimental import pallas as pl
from jax.experimental.pallas import tpu as pltpu
from jax.sharding import PartitionSpec as P

F32 = jnp.float32
BF16 = jnp.bfloat16
BLK = 128
NB = 256
NS = 16
CAP = 32
SLOTS = NS * CAP
CUBES = 128
MOST = 4
SUB = 16
ROWS = 5 * CAP + 8
KF = 32
PITCH = SLOTS + 8

TIME_STEP = 0.2
EARTH_SPIN = 0.0588
J2_COEF = 0.00108263
DRAG_SCALE = 0.008
TABLE_SCALE = 63 / 0.4
SPEED_FLOOR = 0.04


def iota(shape, dim):
    return lax.broadcasted_iota(jnp.int32, shape, dim)


def split2(x):
    high = x.astype(BF16)
    return high, (x - high.astype(F32)).astype(BF16)


def columns_of(row):
    parts = [
        jnp.transpose(jnp.broadcast_to(row[:, k : k + BLK], (BLK, BLK)))
        for k in range(0, row.shape[1], BLK)
    ]
    return jnp.concatenate(parts, axis=0)


def rank_row(row):
    n = row.shape[1]
    column = columns_of(row)
    ranks = []
    for k in range(0, n, BLK):
        earlier = iota((n, BLK), 0) < iota((n, BLK), 1) + k
        same = column == row[:, k : k + BLK]
        ranks.append(jnp.sum(jnp.where(earlier & same, 1.0, 0.0), axis=0, keepdims=True))
    return jnp.concatenate(ranks, axis=1)


def block_slots(cube_row):
    owner = lax.shift_right_logical(cube_row, 7).astype(F32)
    return owner * CAP + rank_row(owner)


def substep(x, y, z, vx, vy, vz, drag, tab, slope):
    r2 = x * x + y * y + z * z
    ri = lax.rsqrt(r2)
    h = r2 * ri - 1.0
    coord = jnp.clip(h * TABLE_SCALE, -1.0, 64.0)
    below = jnp.floor(coord)
    frac = coord - below
    index = below.astype(jnp.int32) + 1
    base = jnp.concatenate(
        [jnp.take_along_axis(tab, index[k : k + 8], axis=1) for k in range(0, x.shape[0], 8)], axis=0
    )
    rise = jnp.concatenate(
        [jnp.take_along_axis(slope, index[k : k + 8], axis=1) for k in range(0, x.shape[0], 8)], axis=0
    )
    density = jnp.exp(base + frac * rise - h * 10.0)
    ux = vx + EARTH_SPIN * y
    uy = vy - EARTH_SPIN * x
    u2 = ux * ux + uy * uy + vz * vz
    speed = u2 * lax.rsqrt(jnp.maximum(u2, 1e-36))
    pull = density * drag * speed
    i2 = ri * ri
    i3 = i2 * ri
    oblate = (1.5 * J2_COEF * TIME_STEP) * (i2 * i3)
    near = TIME_STEP * i3 + oblate * (1.0 - 5.0 * (z * z * i2))
    vx = vx - x * near - pull * ux
    vy = vy - y * near - pull * uy
    vz = vz - z * (near + 2.0 * oblate) - pull * vz
    return x + TIME_STEP * vx, y + TIME_STEP * vy, z + TIME_STEP * vz, vx, vy, vz


def propagate_kernel(chunk, orbit, props, table, cube, next_out, send, rows, prows, state, planes):
    def spread(b, carry):
        col = pl.ds(pl.multiple_of(b * BLK, BLK), BLK)
        at = pl.multiple_of(b * 8, 8)
        rows[pl.ds(at, 6), :] = orbit[:, col]
        prows[pl.ds(at, 3), :] = props[:, col]
        return carry

    lax.fori_loop(0, NB, spread, 0, unroll=8)

    tab = jnp.concatenate([table[...], jnp.zeros((1, 64), F32)], axis=1)
    tab = pltpu.roll(jnp.broadcast_to(tab, (8, BLK)), 1, 1)
    slope = pltpu.roll(tab, BLK - 1, 1) - tab

    def advance(g, carry):
        def load(ref, c):
            return jnp.concatenate(
                [
                    ref[pl.ds(g * (chunk * 8) + k * 8 + c, 8, stride=8), :]
                    for k in range(0, chunk, 8)
                ],
                axis=0,
            )

        at = pl.ds(pl.multiple_of(g * chunk, chunk), chunk)
        now = tuple(load(rows, c) for c in range(6))
        drag = load(prows, 2) * (DRAG_SCALE * TIME_STEP)
        planes[3, at, :] = load(prows, 0)
        planes[4, at, :] = load(prows, 1)
        now = lax.fori_loop(0, SUB, lambda s, v: substep(*v, drag, tab, slope), now, unroll=2)
        for c in range(6):
            for k in range(0, chunk, 8):
                rows[pl.ds(g * (chunk * 8) + k * 8 + c, 8, stride=8), :] = now[c][k : k + 8]
        for c in range(3):
            planes[c, at, :] = now[3 + c]
        return carry

    lax.fori_loop(0, NB // chunk, advance, 0)

    def collect(b, carry):
        col = pl.ds(pl.multiple_of(b * BLK, BLK), BLK)
        next_out[:, col] = rows[pl.ds(pl.multiple_of(b * 8, 8), 6), :]
        return carry

    lax.fori_loop(0, NB, collect, 0, unroll=8)

    slot = block_slots(cube[...])
    pick = jnp.where(slot == iota((SLOTS, NB), 0).astype(F32), 1.0, 0.0).astype(BF16)
    for c in range(5):
        high, low = split2(planes[c])
        got = jnp.dot(pick, jnp.concatenate([high, low], axis=1), preferred_element_type=F32)
        send[:, c * CAP : (c + 1) * CAP, :] = (got[:, :BLK] + got[:, BLK:]).reshape(NS, CAP, BLK)
    local = ((cube[...] & (CUBES - 1)) + 1).astype(F32)
    ids = jnp.dot(pick, columns_of(local).astype(BF16), preferred_element_type=F32)
    id_rows = []
    for q in range(SLOTS // BLK):
        line = jnp.transpose(ids[q * BLK : (q + 1) * BLK])[0:1]
        id_rows.append(jnp.broadcast_to(line, (4, BLK)))
    id_rows = jnp.concatenate(id_rows, axis=0)
    mine = lax.shift_right_logical(iota((NS, BLK), 1), 5) == (iota((NS, BLK), 0) & 3)
    id_rows = jnp.where(mine, id_rows, 0.0)
    id_rows = id_rows + pltpu.roll(id_rows, 64, 1)
    id_rows = id_rows + pltpu.roll(id_rows, 32, 1)
    send[:, 5 * CAP :, :] = jnp.broadcast_to(id_rows[:, None, :], (NS, 8, BLK))


def features(planes):
    v, (rh, rm), (wh, wm) = planes[:3], planes[3], planes[4]
    radius, weight = rh + rm, wh + wm
    full = [h + m for h, m in v]
    norm = full[0] * full[0] + full[1] * full[1] + full[2] * full[2]

    def thirds(x):
        a = x.astype(BF16).astype(F32)
        b = (x - a).astype(BF16).astype(F32)
        return [a, b, x - a - b]

    one = jnp.ones_like(radius)
    left, right = [], []
    for h, m in v:
        left += [h, h, m, m]
        right += [-2.0 * h, -2.0 * m, -2.0 * h, -2.0 * m]
    left += thirds(norm) + [one, one, one]
    right += [one, one, one] + thirds(norm + SPEED_FLOOR)
    p, q, t = weight, weight * radius, weight * radius * radius

    def halves(x):
        a = x.astype(BF16).astype(F32)
        return a, x - a

    (ph, pm), (qh, qm), (th, tm) = halves(p), halves(q), halves(t)
    left += [th, th, tm, 2.0 * qh, 2.0 * qh, 2.0 * qm, ph, ph, pm]
    right += [ph, pm, ph, qh, qm, qh, th, tm, th]
    return left, right


def pair_kernel(recv, back, left, right, rate):
    got = recv[:, 5 * CAP, :]
    mine = lax.shift_right_logical(iota((NS, BLK), 1), 5) == (iota((NS, BLK), 0) & 3)
    got = jnp.where(mine, got, 0.0)
    ids = jnp.concatenate(
        [jnp.sum(got[4 * q : 4 * q + 4], axis=0, keepdims=True) for q in range(4)], axis=1
    )
    place = jnp.where(ids > 0.0, (ids - 1.0) * MOST + rank_row(ids), -1.0)
    pick = jnp.where(place == iota((SLOTS, SLOTS), 0).astype(F32), 1.0, 0.0).astype(BF16)
    planes = []
    for c in range(5):
        plane = recv[:, c * CAP : (c + 1) * CAP, :].reshape(SLOTS, BLK)
        high, low = split2(plane)
        out = jnp.dot(pick, jnp.concatenate([high, low], axis=1), preferred_element_type=F32)
        planes.append((out[:, :BLK], out[:, BLK:]))
    lefts, rights = features(planes)
    zero = jnp.zeros((SLOTS, BLK), F32)
    for f in range(KF):
        left[f * PITCH : f * PITCH + SLOTS, :] = lefts[f] if f < len(lefts) else zero
        right[f * PITCH : f * PITCH + SLOTS, :] = rights[f] if f < len(rights) else zero

    gap_rows = iota((KF, BLK), 0) < 18
    off_diag = iota((BLK, BLK), 0) != iota((BLK, BLK), 1)

    def one_cube(q):
        base = q * MOST
        lhs = jnp.concatenate(
            [left[pl.ds(base + m, KF, stride=PITCH), :].astype(BF16) for m in range(MOST)], axis=1
        )
        row_sums = [None] * MOST
        out = []
        for c in range(MOST):
            r = right[pl.ds(base + c, KF, stride=PITCH), :]
            rhs = jnp.concatenate(
                [jnp.where(gap_rows, r, 0.0), jnp.where(gap_rows, 0.0, r)], axis=1
            ).astype(BF16)
            tiles = lax.dot_general(
                lhs[:, : (c + 1) * BLK], rhs, (((0,), (0,)), ((), ())), preferred_element_type=F32
            )
            total = None
            for a in range(c + 1):
                gap = jnp.maximum(tiles[a * BLK : (a + 1) * BLK, :BLK], SPEED_FLOOR)
                pair = tiles[a * BLK : (a + 1) * BLK, BLK:] * (gap * lax.rsqrt(gap))
                if a == c:
                    pair = jnp.where(off_diag, pair, 0.0)
                else:
                    row_sums[a] = pair if row_sums[a] is None else row_sums[a] + pair
                part = jnp.sum(pair.reshape(16, 8, BLK), axis=0)
                total = part if total is None else total + part
            out.append(total)
        for c in range(MOST):
            total = out[c]
            if row_sums[c] is not None:
                total = total + jnp.sum(jnp.transpose(row_sums[c]).reshape(16, 8, BLK), axis=0)
            rate[pl.ds(base + c, 1), :] = jnp.sum(total, axis=0, keepdims=True) * (1.0 / (MOST * BLK))

    def cubes(q, carry):
        one_cube(q)
        return carry

    lax.fori_loop(0, CUBES, cubes, 0, unroll=8)

    place_col = columns_of(place)
    unpick = jnp.concatenate(
        [
            jnp.where(place_col == (iota((SLOTS, BLK), 1) + k).astype(F32), 1.0, 0.0)
            for k in range(0, SLOTS, BLK)
        ],
        axis=1,
    ).astype(BF16)
    high, low = split2(rate[...])
    out = jnp.dot(unpick, jnp.concatenate([high, low], axis=1), preferred_element_type=F32)
    back[...] = (out[:, :BLK] + out[:, BLK:]).reshape(NS, CAP, BLK)


def unpack_kernel(back, cube, out):
    slot_col = columns_of(block_slots(cube[...]))
    pick = jnp.concatenate(
        [
            jnp.where(slot_col == (iota((NB, BLK), 1) + k).astype(F32), 1.0, 0.0)
            for k in range(0, SLOTS, BLK)
        ],
        axis=1,
    ).astype(BF16)
    high, low = split2(back[...].reshape(SLOTS, BLK))
    got = jnp.dot(pick, jnp.concatenate([high, low], axis=1), preferred_element_type=F32)
    out[...] = got[:, :BLK] + got[:, BLK:]


VMEM = pl.BlockSpec(memory_space=pltpu.VMEM)
PARAMS = pltpu.CompilerParams(vmem_limit_bytes=56 * 2**20)


def propagate_call(orbit_state, object_props, table, cube, chunk=256):
    return pl.pallas_call(
        functools.partial(propagate_kernel, chunk),
        out_shape=(
            jax.ShapeDtypeStruct((6, NB * BLK), F32),
            jax.ShapeDtypeStruct((NS, ROWS, BLK), F32),
        ),
        in_specs=[VMEM] * 4,
        out_specs=(VMEM, VMEM),
        scratch_shapes=[
            pltpu.VMEM((NB * 8, BLK), F32),
            pltpu.VMEM((NB * 8, BLK), F32),
            pltpu.VMEM((8, BLK), F32),
            pltpu.VMEM((5, NB, BLK), F32),
        ],
        compiler_params=PARAMS,
        name="propagate",
    )(orbit_state, object_props, table, cube)


def pair_call(recv):
    return pl.pallas_call(
        pair_kernel,
        out_shape=jax.ShapeDtypeStruct((NS, CAP, BLK), F32),
        in_specs=[VMEM],
        out_specs=VMEM,
        scratch_shapes=[
            pltpu.VMEM((KF * PITCH, BLK), F32),
            pltpu.VMEM((KF * PITCH, BLK), F32),
            pltpu.VMEM((SLOTS, BLK), F32),
        ],
        compiler_params=PARAMS,
        name="pairs",
    )(recv)


def unpack_call(back, cube):
    return pl.pallas_call(
        unpack_kernel,
        out_shape=jax.ShapeDtypeStruct((NB, BLK), F32),
        in_specs=[VMEM] * 2,
        out_specs=VMEM,
        compiler_params=PARAMS,
        name="unpack",
    )(back, cube)


def on_device(orbit_state, object_props, density_table, block_cube):
    cube = block_cube.reshape(1, NB)
    next_state, send = propagate_call(orbit_state, object_props, density_table.reshape(1, 64), cube)
    recv = lax.all_to_all(send, "space", split_axis=0, concat_axis=0, tiled=True)
    back = pair_call(recv)
    home = lax.all_to_all(back, "space", split_axis=0, concat_axis=0, tiled=True)
    return next_state, unpack_call(home, cube).reshape(NB * BLK)


def solution(mesh):
    placed = (P(None, ("mc", "space")), P(None, ("mc", "space")), P(), P(("mc", "space")))
    return jax.shard_map(
        on_device,
        mesh=mesh,
        in_specs=placed,
        out_specs=(P(None, ("mc", "space")), P(("mc", "space"))),
        check_vma=False,
    )
```

```python
import jax
import jax.numpy as jnp
from jax import lax
from jax.experimental import pallas as pl
from jax.experimental.pallas import tpu as pltpu
from jax.sharding import PartitionSpec as P

F32 = jnp.float32
BF16 = jnp.bfloat16
MESH = pl.DeviceIdType.MESH
BLK = 128
NB = 256
NS = 16
CAP = 32
SLOTS = NS * CAP
CUBES = 128
MOST = 4
SUB = 16
GROUP = 8
KF = 32
PITCH = SLOTS + 8

TIME_STEP = 0.2
EARTH_SPIN = 0.0588
J2_COEF = 0.00108263
DRAG_SCALE = 0.008
TABLE_SCALE = 63 / 0.4
SPEED_FLOOR = 0.04


def iota(shape, dim):
    return lax.broadcasted_iota(jnp.int32, shape, dim)


def split2(x):
    high = x.astype(BF16)
    return high, (x - high.astype(F32)).astype(BF16)


def columns_of(row):
    parts = [
        jnp.transpose(jnp.broadcast_to(row[:, k : k + BLK], (BLK, BLK)))
        for k in range(0, row.shape[1], BLK)
    ]
    return jnp.concatenate(parts, axis=0)


def rank_row(row):
    n = row.shape[1]
    column = columns_of(row)
    ranks = []
    for k in range(0, n, BLK):
        earlier = iota((n, BLK), 0) < iota((n, BLK), 1) + k
        same = column == row[:, k : k + BLK]
        ranks.append(jnp.sum(jnp.where(earlier & same, 1.0, 0.0), axis=0, keepdims=True))
    return jnp.concatenate(ranks, axis=1)


def cube_maps(cube_row):
    low, high = cube_row & 15, lax.shift_right_logical(cube_row, 4)
    spread = [(low + f) & 15 for f in (0, high, 5 * high + lax.shift_right_logical(high, 3))]
    owner = lax.shift_right_logical(cube_row, 7)
    return [(owner, cube_row & (CUBES - 1))] + [(to, high) for to in spread]


def substep(x, y, z, vx, vy, vz, drag, tab, slope):
    r2 = x * x + y * y + z * z
    ri = lax.rsqrt(r2)
    h = r2 * ri - 1.0
    coord = jnp.clip(h * TABLE_SCALE, -1.0, 64.0)
    below = jnp.floor(coord)
    frac = coord - below
    index = below.astype(jnp.int32) + 1
    base = jnp.concatenate(
        [jnp.take_along_axis(tab, index[k : k + 8], axis=1) for k in range(0, x.shape[0], 8)], axis=0
    )
    rise = jnp.concatenate(
        [jnp.take_along_axis(slope, index[k : k + 8], axis=1) for k in range(0, x.shape[0], 8)], axis=0
    )
    density = jnp.exp(base + frac * rise - h * 10.0)
    ux = vx + EARTH_SPIN * y
    uy = vy - EARTH_SPIN * x
    u2 = ux * ux + uy * uy + vz * vz
    speed = u2 * lax.rsqrt(jnp.maximum(u2, 1e-36))
    pull = density * drag * speed
    i2 = ri * ri
    i3 = i2 * ri
    oblate = (1.5 * J2_COEF * TIME_STEP) * (i2 * i3)
    near = TIME_STEP * i3 + oblate * (1.0 - 5.0 * (z * z * i2))
    vx = vx - x * near - pull * ux
    vy = vy - y * near - pull * uy
    vz = vz - z * (near + 2.0 * oblate) - pull * vz
    return x + TIME_STEP * vx, y + TIME_STEP * vy, z + TIME_STEP * vz, vx, vy, vz


def hello(me):
    barrier = pltpu.get_barrier_semaphore()

    def tell(k, carry):
        pl.semaphore_signal(
            barrier, inc=1, device_id={"space": lax.rem(me + k, NS)}, device_id_type=MESH
        )
        return carry

    lax.fori_loop(1, NS, tell, 0)
    return barrier


def send_all(me, out_of, into, send_sem, recv_sem):
    def start(k, carry):
        to = lax.rem(me + k, NS)
        pltpu.make_async_remote_copy(
            src_ref=out_of(to),
            dst_ref=into.at[me],
            send_sem=send_sem.at[to],
            recv_sem=recv_sem.at[me],
            device_id={"space": to},
            device_id_type=MESH,
        ).start()
        return carry

    lax.fori_loop(1, NS, start, 0)


def wait_all(me, out_of, into, send_sem, recv_sem):
    def arrive(k, carry):
        other = lax.rem(me + k, NS)
        copy = pltpu.make_async_remote_copy(
            src_ref=out_of(other),
            dst_ref=into.at[other],
            send_sem=send_sem.at[other],
            recv_sem=recv_sem.at[other],
            device_id={"space": other},
            device_id_type=MESH,
        )
        copy.wait_recv()
        copy.wait_send()
        return carry

    lax.fori_loop(1, NS, arrive, 0)


def exchange_kernel(
    orbit_in, props_in, table, cube, next_out, recv_a, recv_b, slot_out,
    orbit, props, rows, prows, planes, need, needs, send_a, send_b,
    local_sem, need_send, need_recv, a_send, a_recv, b_send, b_recv,
):
    me = lax.axis_index("space")
    barrier = hello(me)
    orbit_copy = pltpu.make_async_copy(orbit_in, orbit, local_sem.at[0])
    props_copy = pltpu.make_async_copy(props_in, props, local_sem.at[1])
    orbit_copy.start()
    props_copy.start()

    maps = cube_maps(cube[...])
    slots = []
    for to, _ in maps:
        rank = rank_row(to.astype(F32))
        slots.append((to.astype(F32) * CAP + rank, jnp.max(rank, axis=1, keepdims=True)))
    need[...] = jnp.concatenate(
        [jnp.broadcast_to(most, (1, BLK)) for _, most in slots] + [jnp.zeros((4, BLK), F32)], axis=0
    )
    needs[pl.ds(me, 1)] = need[...][None]
    pl.semaphore_wait(barrier, NS - 1)
    send_all(me, lambda to: need, needs, need_send, need_recv)

    props_copy.wait()
    orbit_copy.wait()

    def spread(b, carry):
        col = pl.ds(pl.multiple_of(b * BLK, BLK), BLK)
        at = pl.multiple_of(b * 8, 8)
        rows[pl.ds(at, 6), :] = orbit[:, col]
        prows[pl.ds(at, 3), :] = props[:, col]
        return carry

    lax.fori_loop(0, NB, spread, 0, unroll=8)

    def load(ref, c):
        return jnp.concatenate(
            [ref[pl.ds(k * 8 + c, 8, stride=8), :] for k in range(0, NB, 8)], axis=0
        )

    wait_all(me, lambda to: need, needs, need_send, need_recv)
    worst = jnp.max(needs[...], axis=0)
    wide = lambda m: jnp.concatenate([worst[m : m + 1]] * 2, axis=1) < CAP
    slot, local = slots[0][0], maps[0][1]
    for m in (3, 2, 1):
        slot = jnp.where(wide(m), slots[m][0], slot)
        local = jnp.where(wide(m), maps[m][1], local)
    slot_out[...] = jnp.broadcast_to(slot, (8, NB))
    pick = jnp.where(slot == iota((SLOTS, NB), 0).astype(F32), 1.0, 0.0).astype(BF16)

    def pack(plane):
        high, low = split2(plane)
        got = jnp.dot(pick, jnp.concatenate([high, low], axis=1), preferred_element_type=F32)
        return (got[:, :BLK] + got[:, BLK:]).reshape(NS, CAP, BLK)

    send_a[:, :CAP, :] = pack(load(prows, 0))
    send_a[:, CAP : 2 * CAP, :] = pack(load(prows, 1))
    ids = jnp.dot(
        pick, columns_of((local + 1).astype(F32)).astype(BF16), preferred_element_type=F32
    )
    id_rows = []
    for q in range(SLOTS // BLK):
        line = jnp.transpose(ids[q * BLK : (q + 1) * BLK])[0:1]
        id_rows.append(jnp.broadcast_to(line, (4, BLK)))
    id_rows = jnp.concatenate(id_rows, axis=0)
    mine = lax.shift_right_logical(iota((NS, BLK), 1), 5) == (iota((NS, BLK), 0) & 3)
    id_rows = jnp.where(mine, id_rows, 0.0)
    id_rows = id_rows + pltpu.roll(id_rows, 64, 1)
    id_rows = id_rows + pltpu.roll(id_rows, 32, 1)
    send_a[:, 2 * CAP :, :] = jnp.broadcast_to(id_rows[:, None, :], (NS, 8, BLK))
    keep_a = pltpu.make_async_copy(send_a.at[me], recv_a.at[me], local_sem.at[2])
    keep_a.start()
    send_all(me, lambda to: send_a.at[to], recv_a, a_send, a_recv)

    tab = jnp.concatenate([table[...], jnp.zeros((1, 64), F32)], axis=1)
    tab = pltpu.roll(jnp.broadcast_to(tab, (8, BLK)), 1, 1)
    slope = pltpu.roll(tab, BLK - 1, 1) - tab
    now = tuple(load(rows, c) for c in range(6))
    drag = load(prows, 2) * (DRAG_SCALE * TIME_STEP)
    now = lax.fori_loop(0, SUB, lambda s, v: substep(*v, drag, tab, slope), now, unroll=2)
    for c in range(6):
        for k in range(0, NB, 8):
            rows[pl.ds(k * 8 + c, 8, stride=8), :] = now[c][k : k + 8]
    for c in range(3):
        planes[c] = now[3 + c]
    for c in range(3):
        send_b[:, c * CAP : (c + 1) * CAP, :] = pack(planes[c])
    keep_b = pltpu.make_async_copy(send_b.at[me], recv_b.at[me], local_sem.at[3])
    keep_b.start()
    send_all(me, lambda to: send_b.at[to], recv_b, b_send, b_recv)

    def collect(b, carry):
        col = pl.ds(pl.multiple_of(b * BLK, BLK), BLK)
        orbit[:, col] = rows[pl.ds(pl.multiple_of(b * 8, 8), 6), :]
        return carry

    lax.fori_loop(0, NB, collect, 0, unroll=8)
    next_copy = pltpu.make_async_copy(orbit, next_out, local_sem.at[0])
    next_copy.start()
    keep_a.wait()
    keep_b.wait()
    wait_all(me, lambda to: send_a.at[to], recv_a, a_send, a_recv)
    wait_all(me, lambda to: send_b.at[to], recv_b, b_send, b_recv)
    next_copy.wait()


def features(planes):
    v, (rh, rm), (wh, wm) = planes[:3], planes[3], planes[4]
    radius, weight = rh + rm, wh + wm
    full = [h + m for h, m in v]
    norm = full[0] * full[0] + full[1] * full[1] + full[2] * full[2]

    def thirds(x):
        a = x.astype(BF16).astype(F32)
        b = (x - a).astype(BF16).astype(F32)
        return [a, b, x - a - b]

    one = jnp.ones_like(radius)
    left, right = [], []
    for h, m in v:
        left += [h, h, m, m]
        right += [-2.0 * h, -2.0 * m, -2.0 * h, -2.0 * m]
    left += thirds(norm) + [one, one, one]
    right += [one, one, one] + thirds(norm + SPEED_FLOOR)
    p, q, t = weight, weight * radius, weight * radius * radius

    def halves(x):
        a = x.astype(BF16).astype(F32)
        return a, x - a

    (ph, pm), (qh, qm), (th, tm) = halves(p), halves(q), halves(t)
    left += [th, th, tm, 2.0 * qh, 2.0 * qh, 2.0 * qm, ph, ph, pm]
    right += [ph, pm, ph, qh, qm, qh, th, tm, th]
    return left, right


def cube_order(ids):
    column = columns_of(ids)
    ranks, counts = [], []
    for k in range(0, SLOTS, BLK):
        same = column == ids[:, k : k + BLK]
        earlier = iota((SLOTS, BLK), 0) < iota((SLOTS, BLK), 1) + k
        ranks.append(jnp.sum(jnp.where(earlier & same, 1.0, 0.0), axis=0, keepdims=True))
        counts.append(jnp.sum(jnp.where(same, 1.0, 0.0), axis=0, keepdims=True))
    rank, count = jnp.concatenate(ranks, axis=1), jnp.concatenate(counts, axis=1)
    key = (MOST - count) * 256.0 + ids
    first = (ids > 0.0) & (rank == 0.0)
    first_keys = columns_of(jnp.where(first, key, 1e9))
    before = [
        jnp.sum(jnp.where(first_keys < key[:, k : k + BLK], 1.0, 0.0), axis=0, keepdims=True)
        for k in range(0, SLOTS, BLK)
    ]
    place = jnp.where(ids > 0.0, jnp.concatenate(before, axis=1) * MOST + rank, -1.0)
    cubes = [
        jnp.sum(jnp.where(first & (count >= n), 1.0, 0.0)).astype(jnp.int32)
        for n in range(MOST, 0, -1)
    ]
    return place, cubes


def pair_kernel(recv_a, recv_b, back, left, right, rate):
    got = recv_a[:, 2 * CAP, :]
    mine = lax.shift_right_logical(iota((NS, BLK), 1), 5) == (iota((NS, BLK), 0) & 3)
    got = jnp.where(mine, got, 0.0)
    ids = jnp.concatenate(
        [jnp.sum(got[4 * q : 4 * q + 4], axis=0, keepdims=True) for q in range(4)], axis=1
    )
    place, cubes = cube_order(ids)
    pick = jnp.where(place == iota((SLOTS, SLOTS), 0).astype(F32), 1.0, 0.0).astype(BF16)
    planes = []
    for ref, c in ((recv_b, 0), (recv_b, 1), (recv_b, 2), (recv_a, 0), (recv_a, 1)):
        plane = ref[:, c * CAP : (c + 1) * CAP, :].reshape(SLOTS, BLK)
        high, low = split2(plane)
        out = jnp.dot(pick, jnp.concatenate([high, low], axis=1), preferred_element_type=F32)
        planes.append((out[:, :BLK], out[:, BLK:]))
    lefts, rights = features(planes)
    zero = jnp.zeros((SLOTS, BLK), F32)
    for f in range(KF):
        left[f * PITCH : f * PITCH + SLOTS, :] = lefts[f] if f < len(lefts) else zero
        right[f * PITCH : f * PITCH + SLOTS, :] = rights[f] if f < len(rights) else zero

    gap_rows = iota((KF, BLK), 0) < 18
    off_diag = iota((BLK, BLK), 0) != iota((BLK, BLK), 1)

    rate[...] = zero

    def one_cube(q, members):
        base = q * MOST
        lhs = jnp.concatenate(
            [left[pl.ds(base + m, KF, stride=PITCH), :].astype(BF16) for m in range(members)], axis=1
        )
        row_sums = [None] * members
        out = []
        for c in range(members):
            r = right[pl.ds(base + c, KF, stride=PITCH), :]
            rhs = jnp.concatenate(
                [jnp.where(gap_rows, r, 0.0), jnp.where(gap_rows, 0.0, r)], axis=1
            ).astype(BF16)
            tiles = lax.dot_general(
                lhs[:, : (c + 1) * BLK], rhs, (((0,), (0,)), ((), ())), preferred_element_type=F32
            )
            total = None
            for a in range(c + 1):
                gap = jnp.maximum(tiles[a * BLK : (a + 1) * BLK, :BLK], SPEED_FLOOR)
                pair = tiles[a * BLK : (a + 1) * BLK, BLK:] * (gap * lax.rsqrt(gap))
                if a == c:
                    pair = jnp.where(off_diag, pair, 0.0)
                else:
                    row_sums[a] = pair if row_sums[a] is None else row_sums[a] + pair
                part = jnp.sum(pair.reshape(16, 8, BLK), axis=0)
                total = part if total is None else total + part
            out.append(total)
        for c in range(members):
            total = out[c]
            if row_sums[c] is not None:
                total = total + jnp.sum(jnp.transpose(row_sums[c]).reshape(16, 8, BLK), axis=0)
            rate[pl.ds(base + c, 1), :] = jnp.sum(total, axis=0, keepdims=True) * (1.0 / (MOST * BLK))

    done = 0
    for members, ahead in zip(range(MOST, 0, -1), cubes):
        upto = lax.div(ahead + (GROUP - 1), GROUP)

        def group(g, carry, members=members):
            for k in range(GROUP):
                one_cube(g * GROUP + k, members)
            return carry

        lax.fori_loop(done, upto, group, 0)
        done = upto

    place_col = columns_of(place)
    unpick = jnp.concatenate(
        [
            jnp.where(place_col == (iota((SLOTS, BLK), 1) + k).astype(F32), 1.0, 0.0)
            for k in range(0, SLOTS, BLK)
        ],
        axis=1,
    ).astype(BF16)
    high, low = split2(rate[...])
    out = jnp.dot(unpick, jnp.concatenate([high, low], axis=1), preferred_element_type=F32)
    back[...] = (out[:, :BLK] + out[:, BLK:]).reshape(NS, CAP, BLK)


def return_kernel(back, slot, out, home, kept_sem, send_sem, recv_sem):
    me = lax.axis_index("space")
    barrier = hello(me)
    slot_col = columns_of(slot[0:1, :])
    pick = jnp.concatenate(
        [
            jnp.where(slot_col == (iota((NB, BLK), 1) + k).astype(F32), 1.0, 0.0)
            for k in range(0, SLOTS, BLK)
        ],
        axis=1,
    ).astype(BF16)
    kept = pltpu.make_async_copy(back.at[me], home.at[me], kept_sem)
    kept.start()
    pl.semaphore_wait(barrier, NS - 1)
    send_all(me, lambda to: back.at[to], home, send_sem, recv_sem)
    kept.wait()
    wait_all(me, lambda to: back.at[to], home, send_sem, recv_sem)
    high, low = split2(home[...].reshape(SLOTS, BLK))
    got = jnp.dot(pick, jnp.concatenate([high, low], axis=1), preferred_element_type=F32)
    out[...] = got[:, :BLK] + got[:, BLK:]


VMEM = pl.BlockSpec(memory_space=pltpu.VMEM)
ANY = pl.BlockSpec(memory_space=pl.ANY)
LIMIT = 56 * 2**20
DMA = pltpu.SemaphoreType.DMA


def exchange_call(orbit_state, object_props, table, cube):
    many = NB * BLK
    return pl.pallas_call(
        exchange_kernel,
        out_shape=(
            jax.ShapeDtypeStruct((6, many), F32),
            jax.ShapeDtypeStruct((NS, 2 * CAP + 8, BLK), F32),
            jax.ShapeDtypeStruct((NS, 3 * CAP, BLK), F32),
            jax.ShapeDtypeStruct((8, NB), F32),
        ),
        in_specs=[ANY, ANY, VMEM, VMEM],
        out_specs=(ANY, ANY, ANY, VMEM),
        scratch_shapes=[
            pltpu.VMEM((6, many), F32),
            pltpu.VMEM((3, many), F32),
            pltpu.VMEM((NB * 8, BLK), F32),
            pltpu.VMEM((NB * 8, BLK), F32),
            pltpu.VMEM((3, NB, BLK), F32),
            pltpu.VMEM((8, BLK), F32),
            pltpu.VMEM((NS, 8, BLK), F32),
            pltpu.VMEM((NS, 2 * CAP + 8, BLK), F32),
            pltpu.VMEM((NS, 3 * CAP, BLK), F32),
            DMA((4,)),
        ]
        + [DMA((NS,))] * 6,
        compiler_params=pltpu.CompilerParams(
            collective_id=0, has_side_effects=True, vmem_limit_bytes=LIMIT
        ),
        name="exchange",
    )(orbit_state, object_props, table, cube)


def pair_call(recv_a, recv_b):
    return pl.pallas_call(
        pair_kernel,
        out_shape=jax.ShapeDtypeStruct((NS, CAP, BLK), F32),
        in_specs=[VMEM, VMEM],
        out_specs=VMEM,
        scratch_shapes=[
            pltpu.VMEM((KF * PITCH, BLK), F32),
            pltpu.VMEM((KF * PITCH, BLK), F32),
            pltpu.VMEM((SLOTS, BLK), F32),
        ],
        compiler_params=pltpu.CompilerParams(vmem_limit_bytes=LIMIT),
        name="pairs",
    )(recv_a, recv_b)


def return_call(back, slot):
    return pl.pallas_call(
        return_kernel,
        out_shape=jax.ShapeDtypeStruct((NB, BLK), F32),
        in_specs=[VMEM, VMEM],
        out_specs=VMEM,
        scratch_shapes=[pltpu.VMEM((NS, CAP, BLK), F32), DMA, DMA((NS,)), DMA((NS,))],
        compiler_params=pltpu.CompilerParams(
            collective_id=1, has_side_effects=True, vmem_limit_bytes=LIMIT
        ),
        name="bring_home",
    )(back, slot)


def on_device(orbit_state, object_props, density_table, block_cube):
    next_state, recv_a, recv_b, slot = exchange_call(
        orbit_state, object_props, density_table.reshape(1, 64), block_cube.reshape(1, NB)
    )
    back = pair_call(recv_a, recv_b)
    return next_state, return_call(back, slot).reshape(NB * BLK)


def solution(mesh):
    placed = (P(None, ("mc", "space")), P(None, ("mc", "space")), P(), P(("mc", "space")))
    return jax.shard_map(
        on_device,
        mesh=mesh,
        in_specs=placed,
        out_specs=(P(None, ("mc", "space")), P(("mc", "space"))),
        check_vma=False,
    )
```

```python
import jax
import jax.numpy as jnp
from jax import lax
from jax.experimental import pallas as pl
from jax.experimental.pallas import tpu as pltpu
from jax.sharding import PartitionSpec as P

F32 = jnp.float32
BF16 = jnp.bfloat16
MESH = pl.DeviceIdType.MESH
BLK = 128
NB = 256
NS = 16
CAP = 32
SLOTS = NS * CAP
CUBES = 128
MOST = 4
SUB = 16
GROUP = 8
KF = 32
PITCH = SLOTS + 8

TIME_STEP = 0.2
EARTH_SPIN = 0.0588
J2_COEF = 0.00108263
DRAG_SCALE = 0.008
TABLE_SCALE = 63 / 0.4
SPEED_FLOOR = 0.04


def iota(shape, dim):
    return lax.broadcasted_iota(jnp.int32, shape, dim)


def split2(x):
    high = x.astype(BF16)
    return high, (x - high.astype(F32)).astype(BF16)


def columns_of(row):
    parts = [
        jnp.transpose(jnp.broadcast_to(row[:, k : k + BLK], (BLK, BLK)))
        for k in range(0, row.shape[1], BLK)
    ]
    return jnp.concatenate(parts, axis=0)


def rank_row(row):
    n = row.shape[1]
    column = columns_of(row)
    ranks = []
    for k in range(0, n, BLK):
        earlier = iota((n, BLK), 0) < iota((n, BLK), 1) + k
        same = column == row[:, k : k + BLK]
        ranks.append(jnp.sum(jnp.where(earlier & same, 1.0, 0.0), axis=0, keepdims=True))
    return jnp.concatenate(ranks, axis=1)


def cube_maps(cube_row):
    low, high = cube_row & 15, lax.shift_right_logical(cube_row, 4)
    spread = [(low + f) & 15 for f in (0, high, 5 * high + lax.shift_right_logical(high, 3))]
    owner = lax.shift_right_logical(cube_row, 7)
    return [(owner, cube_row & (CUBES - 1))] + [(to, high) for to in spread]


def substep(x, y, z, vx, vy, vz, drag, tab, slope):
    r2 = x * x + y * y + z * z
    ri = lax.rsqrt(r2)
    h = r2 * ri - 1.0
    coord = jnp.clip(h * TABLE_SCALE, -1.0, 64.0)
    below = jnp.floor(coord)
    frac = coord - below
    index = below.astype(jnp.int32) + 1
    base = jnp.concatenate(
        [jnp.take_along_axis(tab, index[k : k + 8], axis=1) for k in range(0, x.shape[0], 8)], axis=0
    )
    rise = jnp.concatenate(
        [jnp.take_along_axis(slope, index[k : k + 8], axis=1) for k in range(0, x.shape[0], 8)], axis=0
    )
    density = jnp.exp(base + frac * rise - h * 10.0)
    ux = vx + EARTH_SPIN * y
    uy = vy - EARTH_SPIN * x
    u2 = ux * ux + uy * uy + vz * vz
    speed = u2 * lax.rsqrt(jnp.maximum(u2, 1e-36))
    pull = density * drag * speed
    i2 = ri * ri
    i3 = i2 * ri
    oblate = (1.5 * J2_COEF * TIME_STEP) * (i2 * i3)
    near = TIME_STEP * i3 + oblate * (1.0 - 5.0 * (z * z * i2))
    vx = vx - x * near - pull * ux
    vy = vy - y * near - pull * uy
    vz = vz - z * (near + 2.0 * oblate) - pull * vz
    return x + TIME_STEP * vx, y + TIME_STEP * vy, z + TIME_STEP * vz, vx, vy, vz


def hello(me):
    barrier = pltpu.get_barrier_semaphore()

    def tell(k, carry):
        pl.semaphore_signal(
            barrier, inc=1, device_id={"space": lax.rem(me + k, NS)}, device_id_type=MESH
        )
        return carry

    lax.fori_loop(1, NS, tell, 0)
    return barrier


def send_all(me, out_of, into, send_sem, recv_sem):
    def start(k, carry):
        to = lax.rem(me + k, NS)
        pltpu.make_async_remote_copy(
            src_ref=out_of(to),
            dst_ref=into.at[me],
            send_sem=send_sem.at[to],
            recv_sem=recv_sem.at[me],
            device_id={"space": to},
            device_id_type=MESH,
        ).start()
        return carry

    lax.fori_loop(1, NS, start, 0)


def wait_all(me, out_of, into, send_sem, recv_sem):
    def arrive(k, carry):
        other = lax.rem(me + k, NS)
        copy = pltpu.make_async_remote_copy(
            src_ref=out_of(other),
            dst_ref=into.at[other],
            send_sem=send_sem.at[other],
            recv_sem=recv_sem.at[other],
            device_id={"space": other},
            device_id_type=MESH,
        )
        copy.wait_recv()
        copy.wait_send()
        return carry

    lax.fori_loop(1, NS, arrive, 0)


def one_hot(place, n):
    width = place.shape[1]
    return jnp.where(place == iota((n, width), 0).astype(F32), 1.0, 0.0).astype(BF16)


def one_hot_back(place):
    column = columns_of(place)
    n = place.shape[1]
    parts = [
        jnp.where(column == (iota((n, BLK), 1) + k).astype(F32), 1.0, 0.0)
        for k in range(0, SLOTS, BLK)
    ]
    return jnp.concatenate(parts, axis=1).astype(BF16)


def picked(pick, plane):
    high, low = split2(plane)
    got = jnp.dot(pick, jnp.concatenate([high, low], axis=1), preferred_element_type=F32)
    return got[:, :BLK] + got[:, BLK:]


def exchange_kernel(
    orbit_in, props_in, table, cube, next_out, grouped_out, place_out, count_out, slot_out,
    orbit, props, rows, prows, need, needs, send_a, send_b, recv_a, recv_b, grouped,
    local_sem, group_sem, need_send, need_recv, a_send, a_recv, b_send, b_recv,
):
    me = lax.axis_index("space")
    barrier = hello(me)
    orbit_copy = pltpu.make_async_copy(orbit_in, orbit, local_sem.at[0])
    props_copy = pltpu.make_async_copy(props_in, props, local_sem.at[1])
    props_copy.start()
    orbit_copy.start()

    maps = cube_maps(cube[...])
    most = []
    for to, _ in maps:
        held = jnp.sum(jnp.where(to == iota((NS, NB), 0), 1.0, 0.0), axis=1, keepdims=True)
        most.append(jnp.broadcast_to(jnp.max(held, axis=0, keepdims=True), (1, BLK)))
    need[...] = jnp.concatenate(most + [jnp.zeros((4, BLK), F32)], axis=0)
    needs[pl.ds(me, 1)] = need[...][None]
    pl.semaphore_wait(barrier, NS - 1)
    send_all(me, lambda to: need, needs, need_send, need_recv)

    slots = [to.astype(F32) * CAP + rank_row(to.astype(F32)) for to, _ in maps]
    props_copy.wait()
    orbit_copy.wait()

    def spread(b, carry):
        col = pl.ds(pl.multiple_of(b * BLK, BLK), BLK)
        at = pl.multiple_of(b * 8, 8)
        rows[pl.ds(at, 6), :] = orbit[:, col]
        prows[pl.ds(at, 3), :] = props[:, col]
        return carry

    lax.fori_loop(0, NB, spread, 0, unroll=8)

    def load(ref, c):
        return jnp.concatenate(
            [ref[pl.ds(k * 8 + c, 8, stride=8), :] for k in range(0, NB, 8)], axis=0
        )

    wait_all(me, lambda to: need, needs, need_send, need_recv)
    worst = jnp.max(needs[...], axis=0)
    wide = lambda m: jnp.concatenate([worst[m : m + 1]] * 2, axis=1) <= CAP
    slot, local = slots[0], maps[0][1]
    for m in (3, 2, 1):
        slot = jnp.where(wide(m), slots[m], slot)
        local = jnp.where(wide(m), maps[m][1], local)
    slot_out[...] = jnp.broadcast_to(slot, (8, NB))
    pick = one_hot(slot, SLOTS)
    send_a[:, :CAP, :] = picked(pick, load(prows, 0)).reshape(NS, CAP, BLK)
    send_a[:, CAP : 2 * CAP, :] = picked(pick, load(prows, 1)).reshape(NS, CAP, BLK)
    ids = jnp.dot(
        pick, columns_of((local + 1).astype(F32)).astype(BF16), preferred_element_type=F32
    )
    id_rows = []
    for q in range(SLOTS // BLK):
        line = jnp.transpose(ids[q * BLK : (q + 1) * BLK])[0:1]
        id_rows.append(jnp.broadcast_to(line, (4, BLK)))
    id_rows = jnp.concatenate(id_rows, axis=0)
    mine = lax.shift_right_logical(iota((NS, BLK), 1), 5) == (iota((NS, BLK), 0) & 3)
    id_rows = jnp.where(mine, id_rows, 0.0)
    id_rows = id_rows + pltpu.roll(id_rows, 64, 1)
    id_rows = id_rows + pltpu.roll(id_rows, 32, 1)
    send_a[:, 2 * CAP :, :] = jnp.broadcast_to(id_rows[:, None, :], (NS, 8, BLK))
    send_all(me, lambda to: send_a.at[to], recv_a, a_send, a_recv)
    recv_a[pl.ds(me, 1)] = send_a[pl.ds(me, 1)]

    tab = jnp.concatenate([table[...], jnp.zeros((1, 64), F32)], axis=1)
    tab = pltpu.roll(jnp.broadcast_to(tab, (8, BLK)), 1, 1)
    slope = pltpu.roll(tab, BLK - 1, 1) - tab
    now = tuple(load(rows, c) for c in range(6))
    drag = load(prows, 2) * (DRAG_SCALE * TIME_STEP)
    now = lax.fori_loop(0, SUB, lambda s, v: substep(*v, drag, tab, slope), now, unroll=2)
    for c in range(6):
        for k in range(0, NB, 8):
            rows[pl.ds(k * 8 + c, 8, stride=8), :] = now[c][k : k + 8]
    for c in range(3):
        send_b[c] = picked(pick, load(rows, 3 + c)).reshape(NS, CAP, BLK)
        send_all(me, lambda to: send_b.at[c, to], recv_b.at[c], b_send.at[c], b_recv.at[c])

    def collect(b, carry):
        col = pl.ds(pl.multiple_of(b * BLK, BLK), BLK)
        orbit[:, col] = rows[pl.ds(pl.multiple_of(b * 8, 8), 6), :]
        return carry

    lax.fori_loop(0, NB, collect, 0, unroll=8)
    next_copy = pltpu.make_async_copy(orbit, next_out, local_sem.at[0])
    next_copy.start()
    for c in range(3):
        recv_b[c, pl.ds(me, 1)] = send_b[c, pl.ds(me, 1)]

    wait_all(me, lambda to: send_a.at[to], recv_a, a_send, a_recv)
    got = jnp.where(mine, recv_a[:, 2 * CAP, :], 0.0)
    ids = jnp.concatenate(
        [jnp.sum(got[4 * q : 4 * q + 4], axis=0, keepdims=True) for q in range(4)], axis=1
    )
    place, counts = cube_order(ids)
    place_out[...] = jnp.broadcast_to(place, (8, SLOTS))
    count_out[...] = counts
    pick = one_hot(place, SLOTS)

    def regroup(c, plane):
        grouped[c] = picked(pick, plane.reshape(SLOTS, BLK))
        copy = pltpu.make_async_copy(grouped.at[c], grouped_out.at[c], group_sem.at[c])
        copy.start()
        return copy

    copies = [
        regroup(3, recv_a[:, :CAP, :]),
        regroup(4, recv_a[:, CAP : 2 * CAP, :]),
    ]
    for c in range(3):
        wait_all(me, lambda to: send_b.at[c, to], recv_b.at[c], b_send.at[c], b_recv.at[c])
        copies.append(regroup(c, recv_b[c]))
    for copy in copies:
        copy.wait()
    next_copy.wait()


def features(planes):
    radius, weight = planes[3], planes[4]
    v = []
    for full in planes[:3]:
        high = full.astype(BF16).astype(F32)
        v.append((high, full - high))
    norm = planes[0] * planes[0] + planes[1] * planes[1] + planes[2] * planes[2]

    def thirds(x):
        a = x.astype(BF16).astype(F32)
        b = (x - a).astype(BF16).astype(F32)
        return [a, b, x - a - b]

    one = jnp.ones_like(radius)
    left, right = [], []
    for h, m in v:
        left += [h, h, m, m]
        right += [-2.0 * h, -2.0 * m, -2.0 * h, -2.0 * m]
    left += thirds(norm) + [one, one, one]
    right += [one, one, one] + thirds(norm + SPEED_FLOOR)
    p, q, t = weight, weight * radius, weight * radius * radius

    def halves(x):
        a = x.astype(BF16).astype(F32)
        return a, x - a

    (ph, pm), (qh, qm), (th, tm) = halves(p), halves(q), halves(t)
    left += [th, th, tm, 2.0 * qh, 2.0 * qh, 2.0 * qm, ph, ph, pm]
    right += [ph, pm, ph, qh, qm, qh, th, tm, th]
    return left, right


def cube_order(ids):
    column = columns_of(ids)
    ranks, counts = [], []
    for k in range(0, SLOTS, BLK):
        same = column == ids[:, k : k + BLK]
        earlier = iota((SLOTS, BLK), 0) < iota((SLOTS, BLK), 1) + k
        ranks.append(jnp.sum(jnp.where(earlier & same, 1.0, 0.0), axis=0, keepdims=True))
        counts.append(jnp.sum(jnp.where(same, 1.0, 0.0), axis=0, keepdims=True))
    rank, count = jnp.concatenate(ranks, axis=1), jnp.concatenate(counts, axis=1)
    key = (MOST - count) * 256.0 + ids
    first = (ids > 0.0) & (rank == 0.0)
    first_keys = columns_of(jnp.where(first, key, 1e9))
    before = [
        jnp.sum(jnp.where(first_keys < key[:, k : k + BLK], 1.0, 0.0), axis=0, keepdims=True)
        for k in range(0, SLOTS, BLK)
    ]
    place = jnp.where(ids > 0.0, jnp.concatenate(before, axis=1) * MOST + rank, -1.0)
    cubes = [
        jnp.broadcast_to(
            jnp.sum(jnp.where(first & (count >= n), 1, 0), axis=1, keepdims=True), (1, BLK)
        )
        for n in range(MOST, 0, -1)
    ]
    return place, jnp.concatenate(cubes + [jnp.zeros((4, BLK), jnp.int32)], axis=0)


def pair_kernel(next_in, grouped, counts, next_out, rate, left, right, sem):
    next_copy = pltpu.make_async_copy(next_in, next_out, sem)
    next_copy.start()
    lefts, rights = features([grouped[c] for c in range(5)])
    zero = jnp.zeros((SLOTS, BLK), F32)
    for f in range(KF):
        left[f * PITCH : f * PITCH + SLOTS, :] = lefts[f] if f < len(lefts) else zero
        right[f * PITCH : f * PITCH + SLOTS, :] = rights[f] if f < len(rights) else zero

    gap_rows = iota((KF, BLK), 0) < 18
    off_diag = iota((BLK, BLK), 0) != iota((BLK, BLK), 1)

    rate[...] = zero

    def one_cube(q, members):
        base = q * MOST
        lhs = jnp.concatenate(
            [left[pl.ds(base + m, KF, stride=PITCH), :].astype(BF16) for m in range(members)], axis=1
        )
        row_sums = [None] * members
        out = []
        for c in range(members):
            r = right[pl.ds(base + c, KF, stride=PITCH), :]
            rhs = jnp.concatenate(
                [jnp.where(gap_rows, r, 0.0), jnp.where(gap_rows, 0.0, r)], axis=1
            ).astype(BF16)
            tiles = lax.dot_general(
                lhs[:, : (c + 1) * BLK], rhs, (((0,), (0,)), ((), ())), preferred_element_type=F32
            )
            total = None
            for a in range(c + 1):
                gap = jnp.maximum(tiles[a * BLK : (a + 1) * BLK, :BLK], SPEED_FLOOR)
                pair = tiles[a * BLK : (a + 1) * BLK, BLK:] * (gap * lax.rsqrt(gap))
                if a == c:
                    pair = jnp.where(off_diag, pair, 0.0)
                else:
                    row_sums[a] = pair if row_sums[a] is None else row_sums[a] + pair
                part = jnp.sum(pair.reshape(16, 8, BLK), axis=0)
                total = part if total is None else total + part
            out.append(total)
        for c in range(members):
            total = out[c]
            if row_sums[c] is not None:
                total = total + jnp.sum(jnp.transpose(row_sums[c]).reshape(16, 8, BLK), axis=0)
            rate[pl.ds(base + c, 1), :] = jnp.sum(total, axis=0, keepdims=True) * (1.0 / (MOST * BLK))

    done = 0
    for row, members in enumerate(range(MOST, 0, -1)):
        upto = lax.div(counts[row, 0] + (GROUP - 1), GROUP)

        def group(g, carry, members=members):
            for k in range(GROUP):
                one_cube(g * GROUP + k, members)
            return carry

        lax.fori_loop(done, upto, group, 0)
        done = upto

    next_copy.wait()


def return_kernel(rate, place, slot, out, back, home, send_sem, recv_sem):
    me = lax.axis_index("space")
    barrier = hello(me)
    back[...] = picked(one_hot_back(place[0:1, :]), rate[...]).reshape(NS, CAP, BLK)
    home[pl.ds(me, 1)] = back[pl.ds(me, 1)]
    pl.semaphore_wait(barrier, NS - 1)
    send_all(me, lambda to: back.at[to], home, send_sem, recv_sem)
    pick = one_hot_back(slot[0:1, :])
    wait_all(me, lambda to: back.at[to], home, send_sem, recv_sem)
    out[...] = picked(pick, home[...].reshape(SLOTS, BLK))


VMEM = pl.BlockSpec(memory_space=pltpu.VMEM)
ANY = pl.BlockSpec(memory_space=pl.ANY)
LIMIT = 56 * 2**20
DMA = pltpu.SemaphoreType.DMA


def exchange_call(orbit_state, object_props, table, cube):
    many = NB * BLK
    return pl.pallas_call(
        exchange_kernel,
        out_shape=(
            jax.ShapeDtypeStruct((6, many), F32),
            jax.ShapeDtypeStruct((5, SLOTS, BLK), F32),
            jax.ShapeDtypeStruct((8, SLOTS), F32),
            jax.ShapeDtypeStruct((8, BLK), jnp.int32),
            jax.ShapeDtypeStruct((8, NB), F32),
        ),
        in_specs=[ANY, ANY, VMEM, VMEM],
        out_specs=(ANY, ANY, VMEM, VMEM, VMEM),
        scratch_shapes=[
            pltpu.VMEM((6, many), F32),
            pltpu.VMEM((3, many), F32),
            pltpu.VMEM((NB * 8, BLK), F32),
            pltpu.VMEM((NB * 8, BLK), F32),
            pltpu.VMEM((8, BLK), F32),
            pltpu.VMEM((NS, 8, BLK), F32),
            pltpu.VMEM((NS, 2 * CAP + 8, BLK), F32),
            pltpu.VMEM((3, NS, CAP, BLK), F32),
            pltpu.VMEM((NS, 2 * CAP + 8, BLK), F32),
            pltpu.VMEM((3, NS, CAP, BLK), F32),
            pltpu.VMEM((5, SLOTS, BLK), F32),
            DMA((2,)),
            DMA((5,)),
            DMA((NS,)),
            DMA((NS,)),
            DMA((NS,)),
            DMA((NS,)),
            DMA((3, NS)),
            DMA((3, NS)),
        ],
        compiler_params=pltpu.CompilerParams(
            collective_id=0, has_side_effects=True, vmem_limit_bytes=LIMIT
        ),
        name="exchange",
    )(orbit_state, object_props, table, cube)


def pair_call(next_state, grouped, counts):
    return pl.pallas_call(
        pair_kernel,
        out_shape=(
            jax.ShapeDtypeStruct(next_state.shape, F32),
            jax.ShapeDtypeStruct((SLOTS, BLK), F32),
        ),
        in_specs=[ANY, VMEM, pl.BlockSpec(memory_space=pltpu.SMEM)],
        out_specs=(ANY, VMEM),
        scratch_shapes=[
            pltpu.VMEM((KF * PITCH, BLK), F32),
            pltpu.VMEM((KF * PITCH, BLK), F32),
            DMA,
        ],
        compiler_params=pltpu.CompilerParams(vmem_limit_bytes=LIMIT),
        name="pairs",
    )(next_state, grouped, counts)


def return_call(rate, place, slot):
    return pl.pallas_call(
        return_kernel,
        out_shape=jax.ShapeDtypeStruct((NB, BLK), F32),
        in_specs=[VMEM, VMEM, VMEM],
        out_specs=VMEM,
        scratch_shapes=[
            pltpu.VMEM((NS, CAP, BLK), F32),
            pltpu.VMEM((NS, CAP, BLK), F32),
            DMA((NS,)),
            DMA((NS,)),
        ],
        compiler_params=pltpu.CompilerParams(
            collective_id=1, has_side_effects=True, vmem_limit_bytes=LIMIT
        ),
        name="bring_home",
    )(rate, place, slot)


def on_device(orbit_state, object_props, density_table, block_cube):
    moved, grouped, place, counts, slot = exchange_call(
        orbit_state, object_props, density_table.reshape(1, 64), block_cube.reshape(1, NB)
    )
    next_state, rate = pair_call(moved, grouped, counts)
    return next_state, return_call(rate, place, slot).reshape(NB * BLK)


def solution(mesh):
    placed = (P(None, ("mc", "space")), P(None, ("mc", "space")), P(), P(("mc", "space")))
    return jax.shard_map(
        on_device,
        mesh=mesh,
        in_specs=placed,
        out_specs=(P(None, ("mc", "space")), P(("mc", "space"))),
        check_vma=False,
    )
```

```python
import jax
import jax.numpy as jnp
from jax import lax
from jax.experimental import pallas as pl
from jax.experimental.pallas import tpu as pltpu
from jax.sharding import PartitionSpec as P

F32 = jnp.float32
BF16 = jnp.bfloat16
MESH = pl.DeviceIdType.MESH
BLK = 128
NB = 256
NS = 16
CAP = 32
SLOTS = NS * CAP
CUBES = 128
MOST = 4
SUB = 16
GROUP = 8
KF = 32
PITCH = SLOTS + 8

TIME_STEP = 0.2
EARTH_SPIN = 0.0588
J2_COEF = 0.00108263
DRAG_SCALE = 0.008
TABLE_SCALE = 63 / 0.4
SPEED_FLOOR = 0.04


def iota(shape, dim):
    return lax.broadcasted_iota(jnp.int32, shape, dim)


def split2(x):
    high = x.astype(BF16)
    return high, (x - high.astype(F32)).astype(BF16)


def columns_of(row):
    parts = [
        jnp.transpose(jnp.broadcast_to(row[:, k : k + BLK], (BLK, BLK)))
        for k in range(0, row.shape[1], BLK)
    ]
    return jnp.concatenate(parts, axis=0)


def rank_row(row):
    n = row.shape[1]
    column = columns_of(row)
    ranks = []
    for k in range(0, n, BLK):
        earlier = iota((n, BLK), 0) < iota((n, BLK), 1) + k
        same = column == row[:, k : k + BLK]
        ranks.append(jnp.sum(jnp.where(earlier & same, 1.0, 0.0), axis=0, keepdims=True))
    return jnp.concatenate(ranks, axis=1)


def cube_maps(cube_row):
    low, high = cube_row & 15, lax.shift_right_logical(cube_row, 4)
    spread = [(low + f) & 15 for f in (0, high, 5 * high + lax.shift_right_logical(high, 3))]
    owner = lax.shift_right_logical(cube_row, 7)
    return [(owner, cube_row & (CUBES - 1))] + [(to, high) for to in spread]


def substep(x, y, z, vx, vy, vz, drag, tab, slope):
    r2 = x * x + y * y + z * z
    ri = lax.rsqrt(r2)
    h = r2 * ri - 1.0
    coord = jnp.clip(h * TABLE_SCALE, -1.0, 64.0)
    below = jnp.floor(coord)
    frac = coord - below
    index = below.astype(jnp.int32) + 1
    base = jnp.concatenate(
        [jnp.take_along_axis(tab, index[k : k + 8], axis=1) for k in range(0, x.shape[0], 8)], axis=0
    )
    rise = jnp.concatenate(
        [jnp.take_along_axis(slope, index[k : k + 8], axis=1) for k in range(0, x.shape[0], 8)], axis=0
    )
    density = jnp.exp(base + frac * rise - h * 10.0)
    ux = vx + EARTH_SPIN * y
    uy = vy - EARTH_SPIN * x
    u2 = ux * ux + uy * uy + vz * vz
    speed = u2 * lax.rsqrt(jnp.maximum(u2, 1e-36))
    pull = density * drag * speed
    i2 = ri * ri
    i3 = i2 * ri
    oblate = (1.5 * J2_COEF * TIME_STEP) * (i2 * i3)
    near = TIME_STEP * i3 + oblate * (1.0 - 5.0 * (z * z * i2))
    vx = vx - x * near - pull * ux
    vy = vy - y * near - pull * uy
    vz = vz - z * (near + 2.0 * oblate) - pull * vz
    return x + TIME_STEP * vx, y + TIME_STEP * vy, z + TIME_STEP * vz, vx, vy, vz


def hello(me):
    barrier = pltpu.get_barrier_semaphore()

    def tell(k, carry):
        pl.semaphore_signal(
            barrier, inc=1, device_id={"space": lax.rem(me + k, NS)}, device_id_type=MESH
        )
        return carry

    lax.fori_loop(1, NS, tell, 0)
    return barrier


def send_all(me, out_of, into, send_sem, recv_sem):
    def start(k, carry):
        to = lax.rem(me + k, NS)
        pltpu.make_async_remote_copy(
            src_ref=out_of(to),
            dst_ref=into.at[me],
            send_sem=send_sem.at[to],
            recv_sem=recv_sem.at[me],
            device_id={"space": to},
            device_id_type=MESH,
        ).start()
        return carry

    lax.fori_loop(1, NS, start, 0)


def wait_all(me, out_of, into, send_sem, recv_sem):
    def arrive(k, carry):
        other = lax.rem(me + k, NS)
        copy = pltpu.make_async_remote_copy(
            src_ref=out_of(other),
            dst_ref=into.at[other],
            send_sem=send_sem.at[other],
            recv_sem=recv_sem.at[other],
            device_id={"space": other},
            device_id_type=MESH,
        )
        copy.wait_recv()
        copy.wait_send()
        return carry

    lax.fori_loop(1, NS, arrive, 0)


def one_hot(place, n):
    width = place.shape[1]
    return jnp.where(place == iota((n, width), 0).astype(F32), 1.0, 0.0).astype(BF16)


def one_hot_back(place):
    column = columns_of(place)
    n = place.shape[1]
    parts = [
        jnp.where(column == (iota((n, BLK), 1) + k).astype(F32), 1.0, 0.0)
        for k in range(0, SLOTS, BLK)
    ]
    return jnp.concatenate(parts, axis=1).astype(BF16)


def picked(pick, plane):
    high, low = split2(plane)
    got = jnp.dot(pick, jnp.concatenate([high, low], axis=1), preferred_element_type=F32)
    return got[:, :BLK] + got[:, BLK:]


def exchange_kernel(
    orbit_in, props_in, table, cube, next_out, grouped_out, place_out, count_out, slot_out,
    orbit, props, rows, prows, need, needs, send_a, send_b, recv_a, recv_b, grouped,
    local_sem, group_sem, need_send, need_recv, a_send, a_recv, b_send, b_recv,
):
    me = lax.axis_index("space")
    barrier = hello(me)
    orbit_copy = pltpu.make_async_copy(orbit_in, orbit, local_sem.at[0])
    props_copy = pltpu.make_async_copy(props_in, props, local_sem.at[1])
    props_copy.start()
    orbit_copy.start()

    maps = cube_maps(cube[...])
    most = []
    for to, _ in maps:
        held = jnp.sum(jnp.where(to == iota((NS, NB), 0), 1.0, 0.0), axis=1, keepdims=True)
        most.append(jnp.broadcast_to(jnp.max(held, axis=0, keepdims=True), (1, BLK)))
    need[...] = jnp.concatenate(most + [jnp.zeros((4, BLK), F32)], axis=0)
    needs[pl.ds(me, 1)] = need[...][None]
    pl.semaphore_wait(barrier, NS - 1)
    send_all(me, lambda to: need, needs, need_send, need_recv)

    slots = [to.astype(F32) * CAP + rank_row(to.astype(F32)) for to, _ in maps]
    props_copy.wait()
    orbit_copy.wait()

    def spread(b, carry):
        col = pl.ds(pl.multiple_of(b * BLK, BLK), BLK)
        at = pl.multiple_of(b * 8, 8)
        rows[pl.ds(at, 6), :] = orbit[:, col]
        prows[pl.ds(at, 3), :] = props[:, col]
        return carry

    lax.fori_loop(0, NB, spread, 0, unroll=8)

    def load(ref, c):
        return jnp.concatenate(
            [ref[pl.ds(k * 8 + c, 8, stride=8), :] for k in range(0, NB, 8)], axis=0
        )

    wait_all(me, lambda to: need, needs, need_send, need_recv)
    worst = jnp.max(needs[...], axis=0)
    wide = lambda m: jnp.concatenate([worst[m : m + 1]] * 2, axis=1) <= CAP
    slot, local = slots[0], maps[0][1]
    for m in (3, 2, 1):
        slot = jnp.where(wide(m), slots[m], slot)
        local = jnp.where(wide(m), maps[m][1], local)
    slot_out[...] = jnp.broadcast_to(slot, (8, NB))
    pick = one_hot(slot, SLOTS)
    send_a[:, :CAP, :] = picked(pick, load(prows, 0)).reshape(NS, CAP, BLK)
    send_a[:, CAP : 2 * CAP, :] = picked(pick, load(prows, 1)).reshape(NS, CAP, BLK)
    ids = jnp.dot(
        pick, columns_of((local + 1).astype(F32)).astype(BF16), preferred_element_type=F32
    )
    id_rows = []
    for q in range(SLOTS // BLK):
        line = jnp.transpose(ids[q * BLK : (q + 1) * BLK])[0:1]
        id_rows.append(jnp.broadcast_to(line, (4, BLK)))
    id_rows = jnp.concatenate(id_rows, axis=0)
    mine = lax.shift_right_logical(iota((NS, BLK), 1), 5) == (iota((NS, BLK), 0) & 3)
    id_rows = jnp.where(mine, id_rows, 0.0)
    id_rows = id_rows + pltpu.roll(id_rows, 64, 1)
    id_rows = id_rows + pltpu.roll(id_rows, 32, 1)
    send_a[:, 2 * CAP :, :] = jnp.broadcast_to(id_rows[:, None, :], (NS, 8, BLK))
    send_all(me, lambda to: send_a.at[to], recv_a, a_send, a_recv)
    recv_a[pl.ds(me, 1)] = send_a[pl.ds(me, 1)]

    tab = jnp.concatenate([table[...], jnp.zeros((1, 64), F32)], axis=1)
    tab = pltpu.roll(jnp.broadcast_to(tab, (8, BLK)), 1, 1)
    slope = pltpu.roll(tab, BLK - 1, 1) - tab
    now = tuple(load(rows, c) for c in range(6))
    drag = load(prows, 2) * (DRAG_SCALE * TIME_STEP)
    now = lax.fori_loop(0, SUB, lambda s, v: substep(*v, drag, tab, slope), now, unroll=2)
    for c in range(6):
        for k in range(0, NB, 8):
            rows[pl.ds(k * 8 + c, 8, stride=8), :] = now[c][k : k + 8]
    for c in range(3):
        send_b[c] = picked(pick, load(rows, 3 + c)).reshape(NS, CAP, BLK)
        send_all(me, lambda to: send_b.at[c, to], recv_b.at[c], b_send.at[c], b_recv.at[c])

    def collect(b, carry):
        col = pl.ds(pl.multiple_of(b * BLK, BLK), BLK)
        orbit[:, col] = rows[pl.ds(pl.multiple_of(b * 8, 8), 6), :]
        return carry

    lax.fori_loop(0, NB, collect, 0, unroll=8)
    next_copy = pltpu.make_async_copy(orbit, next_out, local_sem.at[0])
    next_copy.start()
    for c in range(3):
        recv_b[c, pl.ds(me, 1)] = send_b[c, pl.ds(me, 1)]

    wait_all(me, lambda to: send_a.at[to], recv_a, a_send, a_recv)
    got = jnp.where(mine, recv_a[:, 2 * CAP, :], 0.0)
    ids = jnp.concatenate(
        [jnp.sum(got[4 * q : 4 * q + 4], axis=0, keepdims=True) for q in range(4)], axis=1
    )
    place, counts = cube_order(ids)
    place_out[...] = jnp.broadcast_to(place, (8, SLOTS))
    count_out[...] = counts
    pick = one_hot(place, SLOTS)

    def regroup(c, plane):
        grouped[c] = picked(pick, plane.reshape(SLOTS, BLK))
        copy = pltpu.make_async_copy(grouped.at[c], grouped_out.at[c], group_sem.at[c])
        copy.start()
        return copy

    copies = [
        regroup(3, recv_a[:, :CAP, :]),
        regroup(4, recv_a[:, CAP : 2 * CAP, :]),
    ]
    for c in range(3):
        wait_all(me, lambda to: send_b.at[c, to], recv_b.at[c], b_send.at[c], b_recv.at[c])
        copies.append(regroup(c, recv_b[c]))
    for copy in copies:
        copy.wait()
    next_copy.wait()


def features(planes):
    radius, weight = planes[3], planes[4]
    v = []
    for full in planes[:3]:
        high = full.astype(BF16).astype(F32)
        v.append((high, full - high))
    norm = planes[0] * planes[0] + planes[1] * planes[1] + planes[2] * planes[2]

    def thirds(x):
        a = x.astype(BF16).astype(F32)
        b = (x - a).astype(BF16).astype(F32)
        return [a, b, x - a - b]

    one = jnp.ones_like(radius)
    left, right = [], []
    for h, m in v:
        left += [h, h, m, m]
        right += [-2.0 * h, -2.0 * m, -2.0 * h, -2.0 * m]
    left += thirds(norm) + [one, one, one]
    right += [one, one, one] + thirds(norm + SPEED_FLOOR)
    p, q, t = weight, weight * radius, weight * radius * radius

    def halves(x):
        a = x.astype(BF16).astype(F32)
        return a, x - a

    (ph, pm), (qh, qm), (th, tm) = halves(p), halves(q), halves(t)
    left += [th, th, tm, 2.0 * qh, 2.0 * qh, 2.0 * qm, ph, ph, pm]
    right += [ph, pm, ph, qh, qm, qh, th, tm, th]
    return left, right


def cube_order(ids):
    column = columns_of(ids)
    ranks, counts = [], []
    for k in range(0, SLOTS, BLK):
        same = column == ids[:, k : k + BLK]
        earlier = iota((SLOTS, BLK), 0) < iota((SLOTS, BLK), 1) + k
        ranks.append(jnp.sum(jnp.where(earlier & same, 1.0, 0.0), axis=0, keepdims=True))
        counts.append(jnp.sum(jnp.where(same, 1.0, 0.0), axis=0, keepdims=True))
    rank, count = jnp.concatenate(ranks, axis=1), jnp.concatenate(counts, axis=1)
    key = (MOST - count) * 256.0 + ids
    first = (ids > 0.0) & (rank == 0.0)
    first_keys = columns_of(jnp.where(first, key, 1e9))
    before = [
        jnp.sum(jnp.where(first_keys < key[:, k : k + BLK], 1.0, 0.0), axis=0, keepdims=True)
        for k in range(0, SLOTS, BLK)
    ]
    place = jnp.where(ids > 0.0, jnp.concatenate(before, axis=1) * MOST + rank, -1.0)
    cubes = [
        jnp.broadcast_to(
            jnp.sum(jnp.where(first & (count >= n), 1, 0), axis=1, keepdims=True), (1, BLK)
        )
        for n in range(MOST, 0, -1)
    ]
    return place, jnp.concatenate(cubes + [jnp.zeros((4, BLK), jnp.int32)], axis=0)


def pair_kernel(next_in, grouped, counts, next_out, rate, left, right, moved, sem):
    next_load = pltpu.make_async_copy(next_in, moved, sem.at[0])
    next_load.start()
    lefts, rights = features([grouped[c] for c in range(5)])
    zero = jnp.zeros((SLOTS, BLK), F32)
    for f in range(KF):
        left[f * PITCH : f * PITCH + SLOTS, :] = lefts[f] if f < len(lefts) else zero
        right[f * PITCH : f * PITCH + SLOTS, :] = rights[f] if f < len(rights) else zero

    gap_rows = iota((KF, BLK), 0) < 18
    off_diag = iota((BLK, BLK), 0) != iota((BLK, BLK), 1)

    rate[...] = zero
    next_load.wait()
    next_copy = pltpu.make_async_copy(moved, next_out, sem.at[1])
    next_copy.start()

    def one_cube(q, members):
        base = q * MOST
        lhs = jnp.concatenate(
            [left[pl.ds(base + m, KF, stride=PITCH), :].astype(BF16) for m in range(members)], axis=1
        )
        row_sums = [None] * members
        out = []
        for c in range(members):
            r = right[pl.ds(base + c, KF, stride=PITCH), :]
            rhs = jnp.concatenate(
                [jnp.where(gap_rows, r, 0.0), jnp.where(gap_rows, 0.0, r)], axis=1
            ).astype(BF16)
            tiles = lax.dot_general(
                lhs[:, : (c + 1) * BLK], rhs, (((0,), (0,)), ((), ())), preferred_element_type=F32
            )
            total = None
            for a in range(c + 1):
                gap = jnp.maximum(tiles[a * BLK : (a + 1) * BLK, :BLK], SPEED_FLOOR)
                pair = tiles[a * BLK : (a + 1) * BLK, BLK:] * (gap * lax.rsqrt(gap))
                if a == c:
                    pair = jnp.where(off_diag, pair, 0.0)
                else:
                    row_sums[a] = pair if row_sums[a] is None else row_sums[a] + pair
                part = jnp.sum(pair.reshape(16, 8, BLK), axis=0)
                total = part if total is None else total + part
            out.append(total)
        for c in range(members):
            total = out[c]
            if row_sums[c] is not None:
                total = total + jnp.sum(jnp.transpose(row_sums[c]).reshape(16, 8, BLK), axis=0)
            rate[pl.ds(base + c, 1), :] = jnp.sum(total, axis=0, keepdims=True) * (1.0 / (MOST * BLK))

    done = 0
    for row, members in enumerate(range(MOST, 0, -1)):
        upto = lax.div(counts[row, 0] + (GROUP - 1), GROUP)

        def group(g, carry, members=members):
            for k in range(GROUP):
                one_cube(g * GROUP + k, members)
            return carry

        lax.fori_loop(done, upto, group, 0)
        done = upto

    next_copy.wait()


def return_kernel(rate, place, slot, out, back, home, send_sem, recv_sem):
    me = lax.axis_index("space")
    barrier = hello(me)
    back[...] = picked(one_hot_back(place[0:1, :]), rate[...]).reshape(NS, CAP, BLK)
    home[pl.ds(me, 1)] = back[pl.ds(me, 1)]
    pl.semaphore_wait(barrier, NS - 1)
    send_all(me, lambda to: back.at[to], home, send_sem, recv_sem)
    pick = one_hot_back(slot[0:1, :])
    wait_all(me, lambda to: back.at[to], home, send_sem, recv_sem)
    out[...] = picked(pick, home[...].reshape(SLOTS, BLK))


VMEM = pl.BlockSpec(memory_space=pltpu.VMEM)
ANY = pl.BlockSpec(memory_space=pl.ANY)
LIMIT = 56 * 2**20
DMA = pltpu.SemaphoreType.DMA


def exchange_call(orbit_state, object_props, table, cube):
    many = NB * BLK
    return pl.pallas_call(
        exchange_kernel,
        out_shape=(
            jax.ShapeDtypeStruct((6, many), F32),
            jax.ShapeDtypeStruct((5, SLOTS, BLK), F32),
            jax.ShapeDtypeStruct((8, SLOTS), F32),
            jax.ShapeDtypeStruct((8, BLK), jnp.int32),
            jax.ShapeDtypeStruct((8, NB), F32),
        ),
        in_specs=[ANY, ANY, VMEM, VMEM],
        out_specs=(ANY, ANY, VMEM, VMEM, VMEM),
        scratch_shapes=[
            pltpu.VMEM((6, many), F32),
            pltpu.VMEM((3, many), F32),
            pltpu.VMEM((NB * 8, BLK), F32),
            pltpu.VMEM((NB * 8, BLK), F32),
            pltpu.VMEM((8, BLK), F32),
            pltpu.VMEM((NS, 8, BLK), F32),
            pltpu.VMEM((NS, 2 * CAP + 8, BLK), F32),
            pltpu.VMEM((3, NS, CAP, BLK), F32),
            pltpu.VMEM((NS, 2 * CAP + 8, BLK), F32),
            pltpu.VMEM((3, NS, CAP, BLK), F32),
            pltpu.VMEM((5, SLOTS, BLK), F32),
            DMA((2,)),
            DMA((5,)),
            DMA((NS,)),
            DMA((NS,)),
            DMA((NS,)),
            DMA((NS,)),
            DMA((3, NS)),
            DMA((3, NS)),
        ],
        compiler_params=pltpu.CompilerParams(
            collective_id=0, has_side_effects=True, vmem_limit_bytes=LIMIT
        ),
        name="exchange",
    )(orbit_state, object_props, table, cube)


def pair_call(next_state, grouped, counts):
    return pl.pallas_call(
        pair_kernel,
        out_shape=(
            jax.ShapeDtypeStruct(next_state.shape, F32),
            jax.ShapeDtypeStruct((SLOTS, BLK), F32),
        ),
        in_specs=[ANY, VMEM, pl.BlockSpec(memory_space=pltpu.SMEM)],
        out_specs=(ANY, VMEM),
        scratch_shapes=[
            pltpu.VMEM((KF * PITCH, BLK), F32),
            pltpu.VMEM((KF * PITCH, BLK), F32),
            pltpu.VMEM(next_state.shape, F32),
            DMA((2,)),
        ],
        compiler_params=pltpu.CompilerParams(vmem_limit_bytes=LIMIT),
        name="pairs",
    )(next_state, grouped, counts)


def return_call(rate, place, slot):
    return pl.pallas_call(
        return_kernel,
        out_shape=jax.ShapeDtypeStruct((NB, BLK), F32),
        in_specs=[VMEM, VMEM, VMEM],
        out_specs=VMEM,
        scratch_shapes=[
            pltpu.VMEM((NS, CAP, BLK), F32),
            pltpu.VMEM((NS, CAP, BLK), F32),
            DMA((NS,)),
            DMA((NS,)),
        ],
        compiler_params=pltpu.CompilerParams(
            collective_id=1, has_side_effects=True, vmem_limit_bytes=LIMIT
        ),
        name="bring_home",
    )(rate, place, slot)


def on_device(orbit_state, object_props, density_table, block_cube):
    moved, grouped, place, counts, slot = exchange_call(
        orbit_state, object_props, density_table.reshape(1, 64), block_cube.reshape(1, NB)
    )
    next_state, rate = pair_call(moved, grouped, counts)
    return next_state, return_call(rate, place, slot).reshape(NB * BLK)


def solution(mesh):
    placed = (P(None, ("mc", "space")), P(None, ("mc", "space")), P(), P(("mc", "space")))
    return jax.shard_map(
        on_device,
        mesh=mesh,
        in_specs=placed,
        out_specs=(P(None, ("mc", "space")), P(("mc", "space"))),
        check_vma=False,
    )
```

```python
import jax
import jax.numpy as jnp
from jax import lax
from jax.experimental import pallas as pl
from jax.experimental.pallas import tpu as pltpu
from jax.sharding import PartitionSpec as P

F32 = jnp.float32
BF16 = jnp.bfloat16
MESH = pl.DeviceIdType.MESH
BLK = 128
NB = 256
NS = 16
CAP = 32
SLOTS = NS * CAP
CUBES = 128
MOST = 4
SUB = 16
GROUP = 16
KF = 32
PITCH = SLOTS + 8

TIME_STEP = 0.2
EARTH_SPIN = 0.0588
J2_COEF = 0.00108263
DRAG_SCALE = 0.008
TABLE_SCALE = 63 / 0.4
SPEED_FLOOR = 0.04


def iota(shape, dim):
    return lax.broadcasted_iota(jnp.int32, shape, dim)


def split2(x):
    high = x.astype(BF16)
    return high, (x - high.astype(F32)).astype(BF16)


def columns_of(row):
    parts = [
        jnp.transpose(jnp.broadcast_to(row[:, k : k + BLK], (BLK, BLK)))
        for k in range(0, row.shape[1], BLK)
    ]
    return jnp.concatenate(parts, axis=0)


def rank_row(row):
    n = row.shape[1]
    column = columns_of(row)
    ranks = []
    for k in range(0, n, BLK):
        earlier = iota((n, BLK), 0) < iota((n, BLK), 1) + k
        same = column == row[:, k : k + BLK]
        ranks.append(jnp.sum(jnp.where(earlier & same, 1.0, 0.0), axis=0, keepdims=True))
    return jnp.concatenate(ranks, axis=1)


def cube_maps(cube_row):
    low, high = cube_row & 15, lax.shift_right_logical(cube_row, 4)
    spread = [(low + f) & 15 for f in (0, high, 5 * high + lax.shift_right_logical(high, 3))]
    owner = lax.shift_right_logical(cube_row, 7)
    return [(owner, cube_row & (CUBES - 1))] + [(to, high) for to in spread]


def substep(x, y, z, vx, vy, vz, drag, tab, slope):
    r2 = x * x + y * y + z * z
    ri = lax.rsqrt(r2)
    h = r2 * ri - 1.0
    coord = jnp.clip(h * TABLE_SCALE, -1.0, 64.0)
    below = jnp.floor(coord)
    frac = coord - below
    index = below.astype(jnp.int32) + 1
    base = jnp.concatenate(
        [jnp.take_along_axis(tab, index[k : k + 8], axis=1) for k in range(0, x.shape[0], 8)], axis=0
    )
    rise = jnp.concatenate(
        [jnp.take_along_axis(slope, index[k : k + 8], axis=1) for k in range(0, x.shape[0], 8)], axis=0
    )
    density = jnp.exp(base + frac * rise - h * 10.0)
    ux = vx + EARTH_SPIN * y
    uy = vy - EARTH_SPIN * x
    u2 = ux * ux + uy * uy + vz * vz
    speed = u2 * lax.rsqrt(jnp.maximum(u2, 1e-36))
    pull = density * drag * speed
    i2 = ri * ri
    i3 = i2 * ri
    oblate = (1.5 * J2_COEF * TIME_STEP) * (i2 * i3)
    near = TIME_STEP * i3 + oblate * (1.0 - 5.0 * (z * z * i2))
    vx = vx - x * near - pull * ux
    vy = vy - y * near - pull * uy
    vz = vz - z * (near + 2.0 * oblate) - pull * vz
    return x + TIME_STEP * vx, y + TIME_STEP * vy, z + TIME_STEP * vz, vx, vy, vz


def hello(me):
    barrier = pltpu.get_barrier_semaphore()
    for k in range(1, NS):
        pl.semaphore_signal(
            barrier, inc=1, device_id={"space": (me + k) & (NS - 1)}, device_id_type=MESH
        )
    return barrier


def send_all(me, out_of, into, send_sem, recv_sem):
    for k in range(1, NS):
        to = (me + k) & (NS - 1)
        pltpu.make_async_remote_copy(
            src_ref=out_of(to),
            dst_ref=into.at[me],
            send_sem=send_sem,
            recv_sem=recv_sem,
            device_id={"space": to},
            device_id_type=MESH,
        ).start()


def wait_all(into, sem):
    others = into.at[pl.ds(0, NS - 1)]
    pltpu.make_async_copy(others, others, sem).wait()


def one_hot(place, n):
    width = place.shape[1]
    return jnp.where(place == iota((n, width), 0).astype(F32), 1.0, 0.0).astype(BF16)


def one_hot_back(place):
    column = columns_of(place)
    n = place.shape[1]
    parts = [
        jnp.where(column == (iota((n, BLK), 1) + k).astype(F32), 1.0, 0.0)
        for k in range(0, SLOTS, BLK)
    ]
    return jnp.concatenate(parts, axis=1).astype(BF16)


def picked(pick, plane):
    high, low = split2(plane)
    got = jnp.dot(pick, jnp.concatenate([high, low], axis=1), preferred_element_type=F32)
    return got[:, :BLK] + got[:, BLK:]


def exchange_kernel(
    orbit_in, props_in, table, cube, next_out, grouped_out, place_out, count_out, slot_out,
    orbit, props, rows, prows, need, needs, send_a, send_b, recv_a, recv_b, grouped,
    local_sem, group_sem, need_send, need_recv, a_send, a_recv, b_send, b_recv,
):
    me = lax.axis_index("space")
    barrier = hello(me)
    orbit_copy = pltpu.make_async_copy(orbit_in, orbit, local_sem.at[0])
    props_copy = pltpu.make_async_copy(props_in, props, local_sem.at[1])
    props_copy.start()
    orbit_copy.start()

    maps = cube_maps(cube[...])
    most = []
    for to, _ in maps:
        held = jnp.sum(jnp.where(to == iota((NS, NB), 0), 1.0, 0.0), axis=1, keepdims=True)
        most.append(jnp.broadcast_to(jnp.max(held, axis=0, keepdims=True), (1, BLK)))
    need[...] = jnp.concatenate(most + [jnp.zeros((4, BLK), F32)], axis=0)
    needs[pl.ds(me, 1)] = need[...][None]
    pl.semaphore_wait(barrier, NS - 1)
    send_all(me, lambda to: need, needs, need_send, need_recv)

    slots = [to.astype(F32) * CAP + rank_row(to.astype(F32)) for to, _ in maps]
    props_copy.wait()
    orbit_copy.wait()

    def spread(b, carry):
        col = pl.ds(pl.multiple_of(b * BLK, BLK), BLK)
        at = pl.multiple_of(b * 8, 8)
        rows[pl.ds(at, 6), :] = orbit[:, col]
        prows[pl.ds(at, 3), :] = props[:, col]
        return carry

    lax.fori_loop(0, NB, spread, 0, unroll=8)

    def load(ref, c):
        return jnp.concatenate(
            [ref[pl.ds(k * 8 + c, 8, stride=8), :] for k in range(0, NB, 8)], axis=0
        )

    wait_all(needs, need_recv)
    worst = jnp.max(needs[...], axis=0)
    wide = lambda m: jnp.concatenate([worst[m : m + 1]] * 2, axis=1) <= CAP
    slot, local = slots[0], maps[0][1]
    for m in (3, 2, 1):
        slot = jnp.where(wide(m), slots[m], slot)
        local = jnp.where(wide(m), maps[m][1], local)
    slot_out[...] = jnp.broadcast_to(slot, (8, NB))
    pick = one_hot(slot, SLOTS)
    send_a[:, :CAP, :] = picked(pick, load(prows, 0)).reshape(NS, CAP, BLK)
    send_a[:, CAP : 2 * CAP, :] = picked(pick, load(prows, 1)).reshape(NS, CAP, BLK)
    ids = jnp.dot(
        pick, columns_of((local + 1).astype(F32)).astype(BF16), preferred_element_type=F32
    )
    id_rows = []
    for q in range(SLOTS // BLK):
        line = jnp.transpose(ids[q * BLK : (q + 1) * BLK])[0:1]
        id_rows.append(jnp.broadcast_to(line, (4, BLK)))
    id_rows = jnp.concatenate(id_rows, axis=0)
    mine = lax.shift_right_logical(iota((NS, BLK), 1), 5) == (iota((NS, BLK), 0) & 3)
    id_rows = jnp.where(mine, id_rows, 0.0)
    id_rows = id_rows + pltpu.roll(id_rows, 64, 1)
    id_rows = id_rows + pltpu.roll(id_rows, 32, 1)
    send_a[:, 2 * CAP :, :] = jnp.broadcast_to(id_rows[:, None, :], (NS, 8, BLK))
    send_all(me, lambda to: send_a.at[to], recv_a, a_send, a_recv)
    recv_a[pl.ds(me, 1)] = send_a[pl.ds(me, 1)]

    tab = jnp.concatenate([table[...], jnp.zeros((1, 64), F32)], axis=1)
    tab = pltpu.roll(jnp.broadcast_to(tab, (8, BLK)), 1, 1)
    slope = pltpu.roll(tab, BLK - 1, 1) - tab
    now = tuple(load(rows, c) for c in range(6))
    drag = load(prows, 2) * (DRAG_SCALE * TIME_STEP)
    now = lax.fori_loop(0, SUB, lambda s, v: substep(*v, drag, tab, slope), now, unroll=4)
    for c in range(6):
        for k in range(0, NB, 8):
            rows[pl.ds(k * 8 + c, 8, stride=8), :] = now[c][k : k + 8]
    for c in range(3):
        send_b[c] = picked(pick, load(rows, 3 + c)).reshape(NS, CAP, BLK)
        send_all(me, lambda to: send_b.at[c, to], recv_b.at[c], b_send.at[c], b_recv.at[c])

    def collect(b, carry):
        col = pl.ds(pl.multiple_of(b * BLK, BLK), BLK)
        orbit[:, col] = rows[pl.ds(pl.multiple_of(b * 8, 8), 6), :]
        return carry

    lax.fori_loop(0, NB, collect, 0, unroll=8)
    next_copy = pltpu.make_async_copy(orbit, next_out, local_sem.at[0])
    next_copy.start()
    for c in range(3):
        recv_b[c, pl.ds(me, 1)] = send_b[c, pl.ds(me, 1)]

    wait_all(recv_a, a_recv)
    got = jnp.where(mine, recv_a[:, 2 * CAP, :], 0.0)
    ids = jnp.concatenate(
        [jnp.sum(got[4 * q : 4 * q + 4], axis=0, keepdims=True) for q in range(4)], axis=1
    )
    place, counts = cube_order(ids)
    place_out[...] = jnp.broadcast_to(place, (8, SLOTS))
    count_out[...] = counts
    pick = one_hot(place, SLOTS)

    def regroup(c, plane):
        grouped[c] = picked(pick, plane.reshape(SLOTS, BLK))
        copy = pltpu.make_async_copy(grouped.at[c], grouped_out.at[c], group_sem.at[c])
        copy.start()
        return copy

    copies = [
        regroup(3, recv_a[:, :CAP, :]),
        regroup(4, recv_a[:, CAP : 2 * CAP, :]),
    ]
    for c in range(3):
        wait_all(recv_b.at[c], b_recv.at[c])
        copies.append(regroup(c, recv_b[c]))
    wait_all(needs, need_send)
    wait_all(recv_a, a_send)
    for c in range(3):
        wait_all(recv_b.at[c], b_send.at[c])
    for copy in copies:
        copy.wait()
    next_copy.wait()


def features(planes):
    radius, weight = planes[3], planes[4]
    v = []
    for full in planes[:3]:
        high = full.astype(BF16).astype(F32)
        v.append((high, full - high))
    norm = planes[0] * planes[0] + planes[1] * planes[1] + planes[2] * planes[2]

    def thirds(x):
        a = x.astype(BF16).astype(F32)
        b = (x - a).astype(BF16).astype(F32)
        return [a, b, x - a - b]

    one = jnp.ones_like(radius)
    left, right = [], []
    for h, m in v:
        left += [h, h, m, m]
        right += [-2.0 * h, -2.0 * m, -2.0 * h, -2.0 * m]
    left += thirds(norm) + [one, one, one]
    right += [one, one, one] + thirds(norm + SPEED_FLOOR)
    p, q, t = weight, weight * radius, weight * radius * radius

    def halves(x):
        a = x.astype(BF16).astype(F32)
        return a, x - a

    (ph, pm), (qh, qm), (th, tm) = halves(p), halves(q), halves(t)
    left += [th, th, tm, 2.0 * qh, 2.0 * qh, 2.0 * qm, ph, ph, pm]
    right += [ph, pm, ph, qh, qm, qh, th, tm, th]
    return left, right


def cube_order(ids):
    column = columns_of(ids)
    ranks, counts = [], []
    for k in range(0, SLOTS, BLK):
        same = column == ids[:, k : k + BLK]
        earlier = iota((SLOTS, BLK), 0) < iota((SLOTS, BLK), 1) + k
        ranks.append(jnp.sum(jnp.where(earlier & same, 1.0, 0.0), axis=0, keepdims=True))
        counts.append(jnp.sum(jnp.where(same, 1.0, 0.0), axis=0, keepdims=True))
    rank, count = jnp.concatenate(ranks, axis=1), jnp.concatenate(counts, axis=1)
    key = (MOST - count) * 256.0 + ids
    first = (ids > 0.0) & (rank == 0.0)
    first_keys = columns_of(jnp.where(first, key, 1e9))
    before = [
        jnp.sum(jnp.where(first_keys < key[:, k : k + BLK], 1.0, 0.0), axis=0, keepdims=True)
        for k in range(0, SLOTS, BLK)
    ]
    place = jnp.where(ids > 0.0, jnp.concatenate(before, axis=1) * MOST + rank, -1.0)
    cubes = [
        jnp.broadcast_to(
            jnp.sum(jnp.where(first & (count >= n), 1, 0), axis=1, keepdims=True), (1, BLK)
        )
        for n in range(MOST, 0, -1)
    ]
    return place, jnp.concatenate(cubes + [jnp.zeros((4, BLK), jnp.int32)], axis=0)


def pair_kernel(next_in, grouped, counts, next_out, rate, left, right, moved, sem):
    next_load = pltpu.make_async_copy(next_in, moved, sem.at[0])
    next_load.start()
    lefts, rights = features([grouped[c] for c in range(5)])
    zero = jnp.zeros((SLOTS, BLK), F32)
    for f in range(KF):
        left[f * PITCH : f * PITCH + SLOTS, :] = lefts[f] if f < len(lefts) else zero
        right[f * PITCH : f * PITCH + SLOTS, :] = rights[f] if f < len(rights) else zero

    gap_rows = iota((KF, BLK), 0) < 18
    off_diag = iota((BLK, BLK), 0) != iota((BLK, BLK), 1)

    rate[...] = zero
    next_load.wait()
    next_copy = pltpu.make_async_copy(moved, next_out, sem.at[1])
    next_copy.start()

    def one_cube(q, members):
        base = q * MOST
        lhs = jnp.concatenate(
            [left[pl.ds(base + m, KF, stride=PITCH), :].astype(BF16) for m in range(members)], axis=1
        )
        row_sums = [None] * members
        out = []
        for c in range(members):
            r = right[pl.ds(base + c, KF, stride=PITCH), :]
            rhs = jnp.concatenate(
                [jnp.where(gap_rows, r, 0.0), jnp.where(gap_rows, 0.0, r)], axis=1
            ).astype(BF16)
            tiles = lax.dot_general(
                lhs[:, : (c + 1) * BLK], rhs, (((0,), (0,)), ((), ())), preferred_element_type=F32
            )
            total = None
            for a in range(c + 1):
                gap = jnp.maximum(tiles[a * BLK : (a + 1) * BLK, :BLK], SPEED_FLOOR)
                pair = tiles[a * BLK : (a + 1) * BLK, BLK:] * (gap * lax.rsqrt(gap))
                if a == c:
                    pair = jnp.where(off_diag, pair, 0.0)
                else:
                    row_sums[a] = pair if row_sums[a] is None else row_sums[a] + pair
                part = jnp.sum(pair.reshape(16, 8, BLK), axis=0)
                total = part if total is None else total + part
            out.append(total)
        for c in range(members):
            total = out[c]
            if row_sums[c] is not None:
                total = total + jnp.sum(jnp.transpose(row_sums[c]).reshape(16, 8, BLK), axis=0)
            rate[pl.ds(base + c, 1), :] = jnp.sum(total, axis=0, keepdims=True) * (1.0 / (MOST * BLK))

    done = 0
    for row, members in enumerate(range(MOST, 0, -1)):
        upto = lax.div(counts[row, 0] + (GROUP - 1), GROUP)

        def group(g, carry, members=members):
            for k in range(GROUP):
                one_cube(g * GROUP + k, members)
            return carry

        lax.fori_loop(done, upto, group, 0)
        done = upto

    next_copy.wait()


def return_kernel(rate, place, slot, out, back, home, send_sem, recv_sem):
    me = lax.axis_index("space")
    barrier = hello(me)
    back[...] = picked(one_hot_back(place[0:1, :]), rate[...]).reshape(NS, CAP, BLK)
    home[pl.ds(me, 1)] = back[pl.ds(me, 1)]
    pl.semaphore_wait(barrier, NS - 1)
    send_all(me, lambda to: back.at[to], home, send_sem, recv_sem)
    pick = one_hot_back(slot[0:1, :])
    wait_all(home, recv_sem)
    out[...] = picked(pick, home[...].reshape(SLOTS, BLK))
    wait_all(home, send_sem)


VMEM = pl.BlockSpec(memory_space=pltpu.VMEM)
ANY = pl.BlockSpec(memory_space=pl.ANY)
LIMIT = 56 * 2**20
DMA = pltpu.SemaphoreType.DMA


def exchange_call(orbit_state, object_props, table, cube):
    many = NB * BLK
    return pl.pallas_call(
        exchange_kernel,
        out_shape=(
            jax.ShapeDtypeStruct((6, many), F32),
            jax.ShapeDtypeStruct((5, SLOTS, BLK), F32),
            jax.ShapeDtypeStruct((8, SLOTS), F32),
            jax.ShapeDtypeStruct((8, BLK), jnp.int32),
            jax.ShapeDtypeStruct((8, NB), F32),
        ),
        in_specs=[ANY, ANY, VMEM, VMEM],
        out_specs=(ANY, ANY, VMEM, VMEM, VMEM),
        scratch_shapes=[
            pltpu.VMEM((6, many), F32),
            pltpu.VMEM((3, many), F32),
            pltpu.VMEM((NB * 8, BLK), F32),
            pltpu.VMEM((NB * 8, BLK), F32),
            pltpu.VMEM((8, BLK), F32),
            pltpu.VMEM((NS, 8, BLK), F32),
            pltpu.VMEM((NS, 2 * CAP + 8, BLK), F32),
            pltpu.VMEM((3, NS, CAP, BLK), F32),
            pltpu.VMEM((NS, 2 * CAP + 8, BLK), F32),
            pltpu.VMEM((3, NS, CAP, BLK), F32),
            pltpu.VMEM((5, SLOTS, BLK), F32),
            DMA((2,)),
            DMA((5,)),
            DMA,
            DMA,
            DMA,
            DMA,
            DMA((3,)),
            DMA((3,)),
        ],
        compiler_params=pltpu.CompilerParams(
            collective_id=0, has_side_effects=True, vmem_limit_bytes=LIMIT
        ),
        name="exchange",
    )(orbit_state, object_props, table, cube)


def pair_call(next_state, grouped, counts):
    return pl.pallas_call(
        pair_kernel,
        out_shape=(
            jax.ShapeDtypeStruct(next_state.shape, F32),
            jax.ShapeDtypeStruct((SLOTS, BLK), F32),
        ),
        in_specs=[ANY, VMEM, pl.BlockSpec(memory_space=pltpu.SMEM)],
        out_specs=(ANY, VMEM),
        scratch_shapes=[
            pltpu.VMEM((KF * PITCH, BLK), F32),
            pltpu.VMEM((KF * PITCH, BLK), F32),
            pltpu.VMEM(next_state.shape, F32),
            DMA((2,)),
        ],
        compiler_params=pltpu.CompilerParams(vmem_limit_bytes=LIMIT),
        name="pairs",
    )(next_state, grouped, counts)


def return_call(rate, place, slot):
    return pl.pallas_call(
        return_kernel,
        out_shape=jax.ShapeDtypeStruct((NB, BLK), F32),
        in_specs=[VMEM, VMEM, VMEM],
        out_specs=VMEM,
        scratch_shapes=[
            pltpu.VMEM((NS, CAP, BLK), F32),
            pltpu.VMEM((NS, CAP, BLK), F32),
            DMA,
            DMA,
        ],
        compiler_params=pltpu.CompilerParams(
            collective_id=1, has_side_effects=True, vmem_limit_bytes=LIMIT
        ),
        name="bring_home",
    )(rate, place, slot)


def on_device(orbit_state, object_props, density_table, block_cube):
    moved, grouped, place, counts, slot = exchange_call(
        orbit_state, object_props, density_table.reshape(1, 64), block_cube.reshape(1, NB)
    )
    next_state, rate = pair_call(moved, grouped, counts)
    return next_state, return_call(rate, place, slot).reshape(NB * BLK)


def solution(mesh):
    placed = (P(None, ("mc", "space")), P(None, ("mc", "space")), P(), P(("mc", "space")))
    return jax.shard_map(
        on_device,
        mesh=mesh,
        in_specs=placed,
        out_specs=(P(None, ("mc", "space")), P(("mc", "space"))),
        check_vma=False,
    )
```

```python
import functools

import jax
import jax.numpy as jnp
from jax import lax
from jax.experimental import pallas as pl
from jax.experimental.pallas import tpu as pltpu
from jax.sharding import PartitionSpec as P

F32 = jnp.float32
BF16 = jnp.bfloat16
MESH = pl.DeviceIdType.MESH
BLK = 128
NB = 256
NS = 16
CAP = 32
SENT = 25
SLOTS = NS * CAP
CUBES = 128
MOST = 4
SUB = 16
EARLY = 8
GROUP = 16
KF = 32
PITCH = SLOTS + 8

TIME_STEP = 0.2
EARTH_SPIN = 0.0588
J2_COEF = 0.00108263
DRAG_SCALE = 0.008
TABLE_SCALE = 63 / 0.4
SPEED_FLOOR = 0.04


def iota(shape, dim):
    return lax.broadcasted_iota(jnp.int32, shape, dim)


def split2(x):
    high = x.astype(BF16)
    return high, (x - high.astype(F32)).astype(BF16)


def columns_of(row):
    parts = [
        jnp.transpose(jnp.broadcast_to(row[:, k : k + BLK], (BLK, BLK)))
        for k in range(0, row.shape[1], BLK)
    ]
    return jnp.concatenate(parts, axis=0)


def rank_row(row):
    n = row.shape[1]
    column = columns_of(row)
    ranks = []
    for k in range(0, n, BLK):
        earlier = iota((n, BLK), 0) < iota((n, BLK), 1) + k
        same = column == row[:, k : k + BLK]
        ranks.append(jnp.sum(jnp.where(earlier & same, 1.0, 0.0), axis=0, keepdims=True))
    return jnp.concatenate(ranks, axis=1)


def balanced(cube, k):
    high = lax.shift_right_logical(cube, 4)
    return ((cube & 15) + lax.shift_right_logical(high * (37 * k + 11), 4)) & 15


def substep(x, y, z, vx, vy, vz, drag, tab, slope):
    r2 = x * x + y * y + z * z
    ri = lax.rsqrt(r2)
    h = r2 * ri - 1.0
    coord = jnp.clip(h * TABLE_SCALE, -1.0, 64.0)
    below = jnp.floor(coord)
    frac = coord - below
    index = below.astype(jnp.int32) + 1
    base = jnp.concatenate(
        [jnp.take_along_axis(tab, index[k : k + 8], axis=1) for k in range(0, x.shape[0], 8)], axis=0
    )
    rise = jnp.concatenate(
        [jnp.take_along_axis(slope, index[k : k + 8], axis=1) for k in range(0, x.shape[0], 8)], axis=0
    )
    density = jnp.exp(base + frac * rise - h * 10.0)
    ux = vx + EARTH_SPIN * y
    uy = vy - EARTH_SPIN * x
    u2 = ux * ux + uy * uy + vz * vz
    speed = u2 * lax.rsqrt(jnp.maximum(u2, 1e-36))
    pull = density * drag * speed
    i2 = ri * ri
    i3 = i2 * ri
    oblate = (1.5 * J2_COEF * TIME_STEP) * (i2 * i3)
    near = TIME_STEP * i3 + oblate * (1.0 - 5.0 * (z * z * i2))
    vx = vx - x * near - pull * ux
    vy = vy - y * near - pull * uy
    vz = vz - z * (near + 2.0 * oblate) - pull * vz
    return x + TIME_STEP * vx, y + TIME_STEP * vy, z + TIME_STEP * vz, vx, vy, vz


def hello(me):
    barrier = pltpu.get_barrier_semaphore()
    for k in range(1, NS):
        pl.semaphore_signal(
            barrier, inc=1, device_id={"space": (me + k) & (NS - 1)}, device_id_type=MESH
        )
    return barrier


def send_all(me, count, out_of, into, send_sem, recv_sem):
    for k in range(1, NS):
        to = (me + k) & (NS - 1)
        pltpu.make_async_remote_copy(
            src_ref=out_of.at[to, pl.ds(0, count)],
            dst_ref=into.at[me, pl.ds(0, count)],
            send_sem=send_sem,
            recv_sem=recv_sem,
            device_id={"space": to},
            device_id_type=MESH,
        ).start()


def wait_all(count, into, sem):
    others = into.at[pl.ds(0, NS - 1), pl.ds(0, count)]
    pltpu.make_async_copy(others, others, sem).wait()


def one_hot(place, n):
    width = place.shape[1]
    return jnp.where(place == iota((n, width), 0).astype(F32), 1.0, 0.0).astype(BF16)


def one_hot_back(place):
    column = columns_of(place)
    n = place.shape[1]
    parts = [
        jnp.where(column == (iota((n, BLK), 1) + k).astype(F32), 1.0, 0.0)
        for k in range(0, SLOTS, BLK)
    ]
    return jnp.concatenate(parts, axis=1).astype(BF16)


def picked(pick, plane):
    high, low = split2(plane)
    got = jnp.dot(pick, jnp.concatenate([high, low], axis=1), preferred_element_type=F32)
    return got[:, :BLK] + got[:, BLK:]


def exchange_kernel(
    sent, orbit_in, props_in, table, cube, next_out, grouped_out, place_out, count_out, slot_out, found_out,
    orbit, props, rows, prows, need, needs, send_r, send_w, send_b, recv_r, recv_w, recv_b, grouped,
    slot_at, place_at, count_at, local_sem, group_sem, need_send, need_recv, sends, recvs,
):
    me = lax.axis_index("space")
    barrier = hello(me)
    orbit_copy = pltpu.make_async_copy(orbit_in, orbit, local_sem.at[0])
    props_copy = pltpu.make_async_copy(props_in, props, local_sem.at[1])
    props_copy.start()
    orbit_copy.start()

    if sent < CAP:
        column = columns_of(cube[...].astype(F32)).astype(jnp.int32)
        to = balanced(column, iota((NB, BLK), 1))
        most = jnp.zeros((1, BLK), F32)
        for device in range(NS):
            held = jnp.sum(jnp.where(to == device, 1.0, 0.0), axis=0, keepdims=True)
            most = jnp.maximum(most, held)
        need[...] = most
        needs[pl.ds(me, 1)] = need[...][None]
        pl.semaphore_wait(barrier, NS - 1)
        for k in range(1, NS):
            pltpu.make_async_remote_copy(
                src_ref=need,
                dst_ref=needs.at[me],
                send_sem=need_send,
                recv_sem=need_recv,
                device_id={"space": (me + k) & (NS - 1)},
                device_id_type=MESH,
            ).start()
        recv_r[:, sent:, :] = jnp.zeros((NS, CAP - sent, BLK), F32)
        recv_w[:, sent + 1 :, :] = jnp.zeros((NS, CAP - sent - 1, BLK), F32)
        for c in range(3):
            recv_b[c, :, sent:, :] = jnp.zeros((NS, CAP - sent, BLK), F32)
    else:
        pl.semaphore_wait(barrier, NS - 1)

    props_copy.wait()
    orbit_copy.wait()

    def spread(b, carry):
        col = pl.ds(pl.multiple_of(b * BLK, BLK), BLK)
        at = pl.multiple_of(b * 8, 8)
        rows[pl.ds(at, 6), :] = orbit[:, col]
        prows[pl.ds(at, 3), :] = props[:, col]
        return carry

    lax.fori_loop(0, NB, spread, 0, unroll=8)

    def load(ref, c):
        return jnp.concatenate(
            [ref[pl.ds(k * 8 + c, 8, stride=8), :] for k in range(0, NB, 8)], axis=0
        )

    tab = jnp.concatenate([table[...], jnp.zeros((1, 64), F32)], axis=1)
    tab = pltpu.roll(jnp.broadcast_to(tab, (8, BLK)), 1, 1)
    slope = pltpu.roll(tab, BLK - 1, 1) - tab
    now = tuple(load(rows, c) for c in range(6))
    drag = load(prows, 2) * (DRAG_SCALE * TIME_STEP)
    advance = lambda s, v: substep(*v, drag, tab, slope)
    now = lax.fori_loop(0, EARLY, advance, now, unroll=4)
    if sent < CAP:
        wait_all(1, needs, need_recv)
        fits = jnp.max(needs[...], axis=0) <= sent
        lane = iota((1, BLK), 1).astype(F32)
        first = jnp.min(jnp.where(fits, lane, float(BLK)), axis=1, keepdims=True)
        found = first < BLK
        to = balanced(cube[...], jnp.where(found, first, 0.0).astype(jnp.int32))
        local = lax.shift_right_logical(cube[...], 4)
    else:
        found = None
        to = lax.shift_right_logical(cube[...], 7)
        local = cube[...] & (CUBES - 1)
    slot = to.astype(F32) * CAP + rank_row(to.astype(F32))
    slot_at[...] = jnp.broadcast_to(slot, (8, NB))
    slot_copy = pltpu.make_async_copy(slot_at, slot_out, local_sem.at[2])
    slot_copy.start()
    pick = one_hot(slot, SLOTS)
    send_r[...] = picked(pick, load(prows, 0)).reshape(NS, CAP, BLK)
    send_all(me, sent, send_r, recv_r, sends.at[3], recvs.at[3])
    send_w[:, :CAP, :] = picked(pick, load(prows, 1)).reshape(NS, CAP, BLK)
    ids = jnp.dot(
        pick, columns_of((local + 1).astype(F32)).astype(BF16), preferred_element_type=F32
    )
    id_rows = []
    for q in range(SLOTS // BLK):
        line = jnp.transpose(ids[q * BLK : (q + 1) * BLK])[0:1]
        id_rows.append(jnp.broadcast_to(line, (4, BLK)))
    id_rows = jnp.concatenate(id_rows, axis=0)
    mine = lax.shift_right_logical(iota((NS, BLK), 1), 5) == (iota((NS, BLK), 0) & 3)
    id_rows = jnp.where(mine, id_rows, 0.0)
    id_rows = id_rows + pltpu.roll(id_rows, 64, 1)
    id_rows = id_rows + pltpu.roll(id_rows, 32, 1)
    send_w[:, sent : sent + 1, :] = id_rows[:, None, :]
    send_all(me, sent + 1, send_w, recv_w, sends.at[4], recvs.at[4])
    recv_w[pl.ds(me, 1)] = send_w[pl.ds(me, 1)]
    recv_r[pl.ds(me, 1)] = send_r[pl.ds(me, 1)]

    now = lax.fori_loop(EARLY, SUB, advance, now, unroll=4)
    for c in range(6):
        for k in range(0, NB, 8):
            rows[pl.ds(k * 8 + c, 8, stride=8), :] = now[c][k : k + 8]
    for c in range(3):
        send_b[c] = picked(pick, load(rows, 3 + c)).reshape(NS, CAP, BLK)
        send_all(me, sent, send_b.at[c], recv_b.at[c], sends.at[c], recvs.at[c])

    def collect(b, carry):
        col = pl.ds(pl.multiple_of(b * BLK, BLK), BLK)
        orbit[:, col] = rows[pl.ds(pl.multiple_of(b * 8, 8), 6), :]
        return carry

    lax.fori_loop(0, NB, collect, 0, unroll=8)
    next_copy = pltpu.make_async_copy(orbit, next_out, local_sem.at[0])
    next_copy.start()
    for c in range(3):
        recv_b[c, pl.ds(me, 1)] = send_b[c, pl.ds(me, 1)]

    wait_all(sent + 1, recv_w, recvs.at[4])
    got = jnp.where(mine, recv_w[:, sent, :], 0.0)
    ids = jnp.concatenate(
        [jnp.sum(got[4 * q : 4 * q + 4], axis=0, keepdims=True) for q in range(4)], axis=1
    )
    place, counts = cube_order(ids)
    place_at[...] = jnp.broadcast_to(place, (8, SLOTS))
    place_copy = pltpu.make_async_copy(place_at, place_out, local_sem.at[3])
    place_copy.start()
    if found is None:
        count_at[...] = counts
        found_out[0, 0] = jnp.int32(1)
    else:
        found_out[0, 0] = jnp.where(found, 1, 0)[0, 0]
        count_at[...] = jnp.where(found, jnp.minimum(counts, CUBES), 0)
    count_copy = pltpu.make_async_copy(count_at, count_out, local_sem.at[4])
    count_copy.start()
    pick = one_hot(place, SLOTS)

    def regroup(c, plane):
        grouped[c] = picked(pick, plane.reshape(SLOTS, BLK))
        copy = pltpu.make_async_copy(grouped.at[c], grouped_out.at[c], group_sem.at[c])
        copy.start()
        return copy

    copies = [regroup(4, recv_w[:, :CAP, :])]
    wait_all(sent, recv_r, recvs.at[3])
    copies.append(regroup(3, recv_r[...]))
    for c in range(3):
        wait_all(sent, recv_b.at[c], recvs.at[c])
        copies.append(regroup(c, recv_b[c]))
    if sent < CAP:
        wait_all(1, needs, need_send)
    wait_all(sent + 1, recv_w, sends.at[4])
    wait_all(sent, recv_r, sends.at[3])
    for c in range(3):
        wait_all(sent, recv_b.at[c], sends.at[c])
    for copy in copies:
        copy.wait()
    for copy in (slot_copy, place_copy, count_copy, next_copy):
        copy.wait()


def features(planes):
    radius, weight = planes[3], planes[4]
    v = []
    for full in planes[:3]:
        high = full.astype(BF16).astype(F32)
        v.append((high, full - high))
    norm = planes[0] * planes[0] + planes[1] * planes[1] + planes[2] * planes[2]

    def thirds(x):
        a = x.astype(BF16).astype(F32)
        b = (x - a).astype(BF16).astype(F32)
        return [a, b, x - a - b]

    one = jnp.ones_like(radius)
    left, right = [], []
    for h, m in v:
        left += [h, h, m, m]
        right += [-2.0 * h, -2.0 * m, -2.0 * h, -2.0 * m]
    left += thirds(norm) + [one, one, one]
    right += [one, one, one] + thirds(norm + SPEED_FLOOR)
    p, q, t = weight, weight * radius, weight * radius * radius

    def halves(x):
        a = x.astype(BF16).astype(F32)
        return a, x - a

    (ph, pm), (qh, qm), (th, tm) = halves(p), halves(q), halves(t)
    left += [th, th, tm, 2.0 * qh, 2.0 * qh, 2.0 * qm, ph, ph, pm]
    right += [ph, pm, ph, qh, qm, qh, th, tm, th]
    return left, right


def cube_order(ids):
    column = columns_of(ids)
    ranks, counts = [], []
    for k in range(0, SLOTS, BLK):
        same = column == ids[:, k : k + BLK]
        earlier = iota((SLOTS, BLK), 0) < iota((SLOTS, BLK), 1) + k
        ranks.append(jnp.sum(jnp.where(earlier & same, 1.0, 0.0), axis=0, keepdims=True))
        counts.append(jnp.sum(jnp.where(same, 1.0, 0.0), axis=0, keepdims=True))
    rank, count = jnp.concatenate(ranks, axis=1), jnp.concatenate(counts, axis=1)
    key = (MOST - count) * 256.0 + ids
    first = (ids > 0.0) & (rank == 0.0)
    first_keys = columns_of(jnp.where(first, key, 1e9))
    before = [
        jnp.sum(jnp.where(first_keys < key[:, k : k + BLK], 1.0, 0.0), axis=0, keepdims=True)
        for k in range(0, SLOTS, BLK)
    ]
    place = jnp.where(ids > 0.0, jnp.concatenate(before, axis=1) * MOST + rank, -1.0)
    cubes = [
        jnp.broadcast_to(
            jnp.sum(jnp.where(first & (count >= n), 1, 0), axis=1, keepdims=True), (1, BLK)
        )
        for n in range(MOST, 0, -1)
    ]
    return place, jnp.concatenate(cubes + [jnp.zeros((4, BLK), jnp.int32)], axis=0)


def pair_kernel(next_in, grouped, counts, next_out, rate, left, right, moved, sem):
    next_load = pltpu.make_async_copy(next_in, moved, sem.at[0])
    next_load.start()
    lefts, rights = features([grouped[c] for c in range(5)])
    zero = jnp.zeros((SLOTS, BLK), F32)
    for f in range(KF):
        left[f * PITCH : f * PITCH + SLOTS, :] = lefts[f] if f < len(lefts) else zero
        right[f * PITCH : f * PITCH + SLOTS, :] = rights[f] if f < len(rights) else zero

    gap_rows = iota((KF, BLK), 0) < 18
    off_diag = iota((BLK, BLK), 0) != iota((BLK, BLK), 1)

    rate[...] = zero
    next_load.wait()
    next_copy = pltpu.make_async_copy(moved, next_out, sem.at[1])
    next_copy.start()

    def one_cube(q, members):
        base = q * MOST
        lhs = jnp.concatenate(
            [left[pl.ds(base + m, KF, stride=PITCH), :].astype(BF16) for m in range(members)], axis=1
        )
        row_sums = [None] * members
        out = []
        for c in range(members):
            r = right[pl.ds(base + c, KF, stride=PITCH), :]
            rhs = jnp.concatenate(
                [jnp.where(gap_rows, r, 0.0), jnp.where(gap_rows, 0.0, r)], axis=1
            ).astype(BF16)
            tiles = lax.dot_general(
                lhs[:, : (c + 1) * BLK], rhs, (((0,), (0,)), ((), ())), preferred_element_type=F32
            )
            total = None
            for a in range(c + 1):
                gap = jnp.maximum(tiles[a * BLK : (a + 1) * BLK, :BLK], SPEED_FLOOR)
                pair = tiles[a * BLK : (a + 1) * BLK, BLK:] * (gap * lax.rsqrt(gap))
                if a == c:
                    pair = jnp.where(off_diag, pair, 0.0)
                else:
                    row_sums[a] = pair if row_sums[a] is None else row_sums[a] + pair
                part = jnp.sum(pair.reshape(16, 8, BLK), axis=0)
                total = part if total is None else total + part
            out.append(total)
        for c in range(members):
            total = out[c]
            if row_sums[c] is not None:
                total = total + jnp.sum(jnp.transpose(row_sums[c]).reshape(16, 8, BLK), axis=0)
            rate[pl.ds(base + c, 1), :] = jnp.sum(total, axis=0, keepdims=True) * (1.0 / (MOST * BLK))

    done = 0
    for row, members in enumerate(range(MOST, 0, -1)):
        upto = lax.div(counts[row, 0] + (GROUP - 1), GROUP)

        def group(g, carry, members=members):
            for k in range(GROUP):
                one_cube(g * GROUP + k, members)
            return carry

        lax.fori_loop(done, upto, group, 0)
        done = upto

    next_copy.wait()


def return_kernel(sent, rate, place, slot, out, back, home, send_sem, recv_sem):
    me = lax.axis_index("space")
    barrier = hello(me)
    back[...] = picked(one_hot_back(place[0:1, :]), rate[...]).reshape(NS, CAP, BLK)
    if sent < CAP:
        home[:, sent:, :] = jnp.zeros((NS, CAP - sent, BLK), F32)
    home[pl.ds(me, 1)] = back[pl.ds(me, 1)]
    pl.semaphore_wait(barrier, NS - 1)
    send_all(me, sent, back, home, send_sem, recv_sem)
    pick = one_hot_back(slot[0:1, :])
    wait_all(sent, home, recv_sem)
    out[...] = picked(pick, home[...].reshape(SLOTS, BLK))
    wait_all(sent, home, send_sem)


VMEM = pl.BlockSpec(memory_space=pltpu.VMEM)
ANY = pl.BlockSpec(memory_space=pl.ANY)
SMEM = pl.BlockSpec(memory_space=pltpu.SMEM)
LIMIT = 56 * 2**20
DMA = pltpu.SemaphoreType.DMA


def exchange_call(sent, orbit_state, object_props, table, cube):
    many = NB * BLK
    wide = pltpu.VMEM((NS, CAP if sent < CAP else CAP + 8, BLK), F32)
    return pl.pallas_call(
        functools.partial(exchange_kernel, sent),
        out_shape=(
            jax.ShapeDtypeStruct((6, many), F32),
            jax.ShapeDtypeStruct((5, SLOTS, BLK), F32),
            jax.ShapeDtypeStruct((8, SLOTS), F32),
            jax.ShapeDtypeStruct((8, BLK), jnp.int32),
            jax.ShapeDtypeStruct((8, NB), F32),
            jax.ShapeDtypeStruct((1, 1), jnp.int32),
        ),
        in_specs=[ANY, ANY, VMEM, VMEM],
        out_specs=(ANY, ANY, ANY, ANY, ANY, SMEM),
        scratch_shapes=[
            pltpu.VMEM((6, many), F32),
            pltpu.VMEM((3, many), F32),
            pltpu.VMEM((NB * 8, BLK), F32),
            pltpu.VMEM((NB * 8, BLK), F32),
            pltpu.VMEM((1, BLK), F32),
            pltpu.VMEM((NS, 1, BLK), F32),
            pltpu.VMEM((NS, CAP, BLK), F32),
            wide,
            pltpu.VMEM((3, NS, CAP, BLK), F32),
            pltpu.VMEM((NS, CAP, BLK), F32),
            wide,
            pltpu.VMEM((3, NS, CAP, BLK), F32),
            pltpu.VMEM((5, SLOTS, BLK), F32),
            pltpu.VMEM((8, NB), F32),
            pltpu.VMEM((8, SLOTS), F32),
            pltpu.VMEM((8, BLK), jnp.int32),
            DMA((5,)),
            DMA((5,)),
            DMA,
            DMA,
            DMA((5,)),
            DMA((5,)),
        ],
        compiler_params=pltpu.CompilerParams(
            collective_id=0 if sent < CAP else 2, has_side_effects=True, vmem_limit_bytes=LIMIT
        ),
        name="exchange",
    )(orbit_state, object_props, table, cube)


def pair_call(next_state, grouped, counts):
    return pl.pallas_call(
        pair_kernel,
        out_shape=(
            jax.ShapeDtypeStruct(next_state.shape, F32),
            jax.ShapeDtypeStruct((SLOTS, BLK), F32),
        ),
        in_specs=[ANY, VMEM, SMEM],
        out_specs=(ANY, VMEM),
        scratch_shapes=[
            pltpu.VMEM((KF * PITCH, BLK), F32),
            pltpu.VMEM((KF * PITCH, BLK), F32),
            pltpu.VMEM(next_state.shape, F32),
            DMA((2,)),
        ],
        compiler_params=pltpu.CompilerParams(vmem_limit_bytes=LIMIT),
        name="pairs",
    )(next_state, grouped, counts)


def return_call(sent, rate, place, slot):
    return pl.pallas_call(
        functools.partial(return_kernel, sent),
        out_shape=jax.ShapeDtypeStruct((NB, BLK), F32),
        in_specs=[VMEM, VMEM, VMEM],
        out_specs=VMEM,
        scratch_shapes=[
            pltpu.VMEM((NS, CAP, BLK), F32),
            pltpu.VMEM((NS, CAP, BLK), F32),
            DMA,
            DMA,
        ],
        compiler_params=pltpu.CompilerParams(
            collective_id=1 if sent < CAP else 3, has_side_effects=True, vmem_limit_bytes=LIMIT
        ),
        name="bring_home",
    )(rate, place, slot)


def on_device(orbit_state, object_props, density_table, block_cube):
    args = (orbit_state, object_props, density_table.reshape(1, 64), block_cube.reshape(1, NB))

    def attempt(sent):
        moved, grouped, place, counts, slot, found = exchange_call(sent, *args)
        next_state, rate = pair_call(moved, grouped, counts)
        return next_state, return_call(sent, rate, place, slot), found.reshape(())

    def again(carry):
        return (attempt(CAP)[1], jnp.int32(1))

    next_state, rate, found = attempt(SENT)
    rate, _ = lax.while_loop(lambda carry: carry[1] == 0, again, (rate, found))
    return next_state, rate.reshape(NB * BLK)


def solution(mesh):
    placed = (P(None, ("mc", "space")), P(None, ("mc", "space")), P(), P(("mc", "space")))
    return jax.shard_map(
        on_device,
        mesh=mesh,
        in_specs=placed,
        out_specs=(P(None, ("mc", "space")), P(("mc", "space"))),
        check_vma=False,
    )
```

```python
import functools

import jax
import jax.numpy as jnp
from jax import lax
from jax.experimental import pallas as pl
from jax.experimental.pallas import tpu as pltpu
from jax.sharding import PartitionSpec as P

F32 = jnp.float32
BF16 = jnp.bfloat16
MESH = pl.DeviceIdType.MESH
BLK = 128
NB = 256
NS = 16
CAP = 32
SENT = 25
SLOTS = NS * CAP
CUBES = 128
MOST = 4
NTAB = 64
SUB = 16
EARLY = 8
GROUP = 16
KF = 32
PITCH = SLOTS + 8

TIME_STEP = 0.2
EARTH_SPIN = 0.0588
J2_COEF = 0.00108263
DRAG_SCALE = 0.008
TABLE_SCALE = 63 / 0.4
SPEED_FLOOR = 0.04


def iota(shape, dim):
    return lax.broadcasted_iota(jnp.int32, shape, dim)


def split2(x):
    high = x.astype(BF16)
    return high, (x - high.astype(F32)).astype(BF16)


def columns_of(row):
    parts = [
        jnp.transpose(jnp.broadcast_to(row[:, k : k + BLK], (BLK, BLK)))
        for k in range(0, row.shape[1], BLK)
    ]
    return jnp.concatenate(parts, axis=0)


def rank_row(row):
    n = row.shape[1]
    column = columns_of(row)
    ranks = []
    for k in range(0, n, BLK):
        earlier = iota((n, BLK), 0) < iota((n, BLK), 1) + k
        same = column == row[:, k : k + BLK]
        ranks.append(jnp.sum(jnp.where(earlier & same, 1.0, 0.0), axis=0, keepdims=True))
    return jnp.concatenate(ranks, axis=1)


def balanced(cube, k):
    high = lax.shift_right_logical(cube, 4)
    return ((cube & 15) + lax.shift_right_logical(high * (37 * k + 11), 4)) & 15


def substep(x, y, z, vx, vy, vz, drag, tab, slope):
    r2 = x * x + y * y + z * z
    ri = lax.rsqrt(r2)
    h = r2 * ri - 1.0
    coord = jnp.clip(h * TABLE_SCALE, -1.0, 64.0)
    below = jnp.floor(coord)
    frac = coord - below
    index = below.astype(jnp.int32) + 1
    base = jnp.concatenate(
        [jnp.take_along_axis(tab, index[k : k + 8], axis=1) for k in range(0, x.shape[0], 8)], axis=0
    )
    rise = jnp.concatenate(
        [jnp.take_along_axis(slope, index[k : k + 8], axis=1) for k in range(0, x.shape[0], 8)], axis=0
    )
    density = jnp.exp(base + frac * rise - h * 10.0)
    ux = vx + EARTH_SPIN * y
    uy = vy - EARTH_SPIN * x
    u2 = ux * ux + uy * uy + vz * vz
    speed = u2 * lax.rsqrt(jnp.maximum(u2, 1e-36))
    pull = density * drag * speed
    i2 = ri * ri
    i3 = i2 * ri
    oblate = (1.5 * J2_COEF * TIME_STEP) * (i2 * i3)
    near = TIME_STEP * i3 + oblate * (1.0 - 5.0 * (z * z * i2))
    vx = vx - x * near - pull * ux
    vy = vy - y * near - pull * uy
    vz = vz - z * (near + 2.0 * oblate) - pull * vz
    return x + TIME_STEP * vx, y + TIME_STEP * vy, z + TIME_STEP * vz, vx, vy, vz


def hello(me):
    barrier = pltpu.get_barrier_semaphore()
    for k in range(1, NS):
        pl.semaphore_signal(
            barrier, inc=1, device_id={"space": (me + k) & (NS - 1)}, device_id_type=MESH
        )
    return barrier


def send_all(me, count, out_of, into, send_sem, recv_sem):
    for k in range(1, NS):
        to = (me + k) & (NS - 1)
        pltpu.make_async_remote_copy(
            src_ref=out_of.at[to, pl.ds(0, count)],
            dst_ref=into.at[me, pl.ds(0, count)],
            send_sem=send_sem,
            recv_sem=recv_sem,
            device_id={"space": to},
            device_id_type=MESH,
        ).start()


def wait_all(count, into, sem):
    others = into.at[pl.ds(0, NS - 1), pl.ds(0, count)]
    pltpu.make_async_copy(others, others, sem).wait()


def one_hot(place, n):
    width = place.shape[1]
    return jnp.where(place == iota((n, width), 0).astype(F32), 1.0, 0.0).astype(BF16)


def one_hot_back(place):
    column = columns_of(place)
    n = place.shape[1]
    parts = [
        jnp.where(column == (iota((n, BLK), 1) + k).astype(F32), 1.0, 0.0)
        for k in range(0, SLOTS, BLK)
    ]
    return jnp.concatenate(parts, axis=1).astype(BF16)


def picked(pick, plane):
    high, low = split2(plane)
    got = jnp.dot(pick, jnp.concatenate([high, low], axis=1), preferred_element_type=F32)
    return got[:, :BLK] + got[:, BLK:]


def exchange_kernel(
    sent, orbit_in, props_in, table_in, cube_in, next_out, grouped_out, place_out, count_out, slot_out, found_out,
    orbit, props, rows, prows, need, needs, send_r, send_w, send_b, recv_r, recv_w, recv_b, grouped,
    slot_at, place_at, count_at, table, cube, local_sem, group_sem, need_send, need_recv, sends, recvs,
):
    me = lax.axis_index("space")
    cube_copy = pltpu.make_async_copy(cube_in, cube, local_sem.at[5])
    table_copy = pltpu.make_async_copy(table_in, table, local_sem.at[6])
    cube_copy.start()
    barrier = hello(me)
    table_copy.start()
    orbit_copy = pltpu.make_async_copy(orbit_in, orbit, local_sem.at[0])
    props_copy = pltpu.make_async_copy(props_in, props, local_sem.at[1])
    props_copy.start()
    orbit_copy.start()
    cube_copy.wait()

    if sent < CAP:
        column = columns_of(cube[...].astype(F32)).astype(jnp.int32)
        to = balanced(column, iota((NB, BLK), 1))
        most = jnp.zeros((1, BLK), F32)
        for device in range(NS):
            held = jnp.sum(jnp.where(to == device, 1.0, 0.0), axis=0, keepdims=True)
            most = jnp.maximum(most, held)
        need[...] = most
        needs[pl.ds(me, 1)] = need[...][None]
        pl.semaphore_wait(barrier, NS - 1)
        for k in range(1, NS):
            pltpu.make_async_remote_copy(
                src_ref=need,
                dst_ref=needs.at[me],
                send_sem=need_send,
                recv_sem=need_recv,
                device_id={"space": (me + k) & (NS - 1)},
                device_id_type=MESH,
            ).start()
        recv_r[:, sent:, :] = jnp.zeros((NS, CAP - sent, BLK), F32)
        recv_w[:, sent + 1 :, :] = jnp.zeros((NS, CAP - sent - 1, BLK), F32)
        for c in range(3):
            recv_b[c, :, sent:, :] = jnp.zeros((NS, CAP - sent, BLK), F32)
    else:
        pl.semaphore_wait(barrier, NS - 1)

    table_copy.wait()
    props_copy.wait()
    orbit_copy.wait()

    def spread(b, carry):
        col = pl.ds(pl.multiple_of(b * BLK, BLK), BLK)
        at = pl.multiple_of(b * 8, 8)
        rows[pl.ds(at, 6), :] = orbit[:, col]
        prows[pl.ds(at, 3), :] = props[:, col]
        return carry

    lax.fori_loop(0, NB, spread, 0, unroll=8)

    def load(ref, c):
        return jnp.concatenate(
            [ref[pl.ds(k * 8 + c, 8, stride=8), :] for k in range(0, NB, 8)], axis=0
        )

    tab = jnp.concatenate([table[...], jnp.zeros((1, 64), F32)], axis=1)
    tab = pltpu.roll(jnp.broadcast_to(tab, (8, BLK)), 1, 1)
    slope = pltpu.roll(tab, BLK - 1, 1) - tab
    now = tuple(load(rows, c) for c in range(6))
    drag = load(prows, 2) * (DRAG_SCALE * TIME_STEP)
    advance = lambda s, v: substep(*v, drag, tab, slope)
    now = lax.fori_loop(0, EARLY, advance, now, unroll=4)
    if sent < CAP:
        wait_all(1, needs, need_recv)
        fits = jnp.max(needs[...], axis=0) <= sent
        lane = iota((1, BLK), 1).astype(F32)
        first = jnp.min(jnp.where(fits, lane, float(BLK)), axis=1, keepdims=True)
        found = first < BLK
        to = balanced(cube[...], jnp.where(found, first, 0.0).astype(jnp.int32))
        local = lax.shift_right_logical(cube[...], 4)
    else:
        found = None
        to = lax.shift_right_logical(cube[...], 7)
        local = cube[...] & (CUBES - 1)
    slot = to.astype(F32) * CAP + rank_row(to.astype(F32))
    slot_at[...] = jnp.broadcast_to(slot, (8, NB))
    slot_copy = pltpu.make_async_copy(slot_at, slot_out, local_sem.at[2])
    slot_copy.start()
    pick = one_hot(slot, SLOTS)
    send_r[...] = picked(pick, load(prows, 0)).reshape(NS, CAP, BLK)
    send_all(me, sent, send_r, recv_r, sends.at[3], recvs.at[3])
    send_w[:, :CAP, :] = picked(pick, load(prows, 1)).reshape(NS, CAP, BLK)
    ids = jnp.dot(
        pick, columns_of((local + 1).astype(F32)).astype(BF16), preferred_element_type=F32
    )
    id_rows = []
    for q in range(SLOTS // BLK):
        line = jnp.transpose(ids[q * BLK : (q + 1) * BLK])[0:1]
        id_rows.append(jnp.broadcast_to(line, (4, BLK)))
    id_rows = jnp.concatenate(id_rows, axis=0)
    mine = lax.shift_right_logical(iota((NS, BLK), 1), 5) == (iota((NS, BLK), 0) & 3)
    id_rows = jnp.where(mine, id_rows, 0.0)
    id_rows = id_rows + pltpu.roll(id_rows, 64, 1)
    id_rows = id_rows + pltpu.roll(id_rows, 32, 1)
    send_w[:, sent : sent + 1, :] = id_rows[:, None, :]
    send_all(me, sent + 1, send_w, recv_w, sends.at[4], recvs.at[4])
    recv_w[pl.ds(me, 1)] = send_w[pl.ds(me, 1)]
    recv_r[pl.ds(me, 1)] = send_r[pl.ds(me, 1)]

    now = lax.fori_loop(EARLY, SUB, advance, now, unroll=4)
    for c in range(6):
        for k in range(0, NB, 8):
            rows[pl.ds(k * 8 + c, 8, stride=8), :] = now[c][k : k + 8]
    for c in range(3):
        send_b[c] = picked(pick, load(rows, 3 + c)).reshape(NS, CAP, BLK)
        send_all(me, sent, send_b.at[c], recv_b.at[c], sends.at[c], recvs.at[c])

    def collect(b, carry):
        col = pl.ds(pl.multiple_of(b * BLK, BLK), BLK)
        orbit[:, col] = rows[pl.ds(pl.multiple_of(b * 8, 8), 6), :]
        return carry

    lax.fori_loop(0, NB, collect, 0, unroll=8)
    next_copy = pltpu.make_async_copy(orbit, next_out, local_sem.at[0])
    next_copy.start()
    for c in range(3):
        recv_b[c, pl.ds(me, 1)] = send_b[c, pl.ds(me, 1)]

    wait_all(sent + 1, recv_w, recvs.at[4])
    got = jnp.where(mine, recv_w[:, sent, :], 0.0)
    ids = jnp.concatenate(
        [jnp.sum(got[4 * q : 4 * q + 4], axis=0, keepdims=True) for q in range(4)], axis=1
    )
    place, counts = cube_order(ids)
    place_at[...] = jnp.broadcast_to(place, (8, SLOTS))
    place_copy = pltpu.make_async_copy(place_at, place_out, local_sem.at[3])
    place_copy.start()
    if found is None:
        count_at[...] = counts
        found_out[0, 0] = jnp.int32(1)
    else:
        found_out[0, 0] = jnp.where(found, 1, 0)[0, 0]
        count_at[...] = jnp.where(found, jnp.minimum(counts, CUBES), 0)
    count_copy = pltpu.make_async_copy(count_at, count_out, local_sem.at[4])
    count_copy.start()
    pick = one_hot(place, SLOTS)

    def regroup(c, plane):
        grouped[c] = picked(pick, plane.reshape(SLOTS, BLK))
        copy = pltpu.make_async_copy(grouped.at[c], grouped_out.at[c], group_sem.at[c])
        copy.start()
        return copy

    copies = [regroup(4, recv_w[:, :CAP, :])]
    wait_all(sent, recv_r, recvs.at[3])
    copies.append(regroup(3, recv_r[...]))
    for c in range(3):
        wait_all(sent, recv_b.at[c], recvs.at[c])
        copies.append(regroup(c, recv_b[c]))
    if sent < CAP:
        wait_all(1, needs, need_send)
    wait_all(sent + 1, recv_w, sends.at[4])
    wait_all(sent, recv_r, sends.at[3])
    for c in range(3):
        wait_all(sent, recv_b.at[c], sends.at[c])
    for copy in copies:
        copy.wait()
    for copy in (slot_copy, place_copy, count_copy, next_copy):
        copy.wait()


def features(planes):
    radius, weight = planes[3], planes[4]
    v = []
    for full in planes[:3]:
        high = full.astype(BF16).astype(F32)
        v.append((high, full - high))
    norm = planes[0] * planes[0] + planes[1] * planes[1] + planes[2] * planes[2]

    def thirds(x):
        a = x.astype(BF16).astype(F32)
        b = (x - a).astype(BF16).astype(F32)
        return [a, b, x - a - b]

    one = jnp.ones_like(radius)
    left, right = [], []
    for h, m in v:
        left += [h, h, m, m]
        right += [-2.0 * h, -2.0 * m, -2.0 * h, -2.0 * m]
    left += thirds(norm) + [one, one, one]
    right += [one, one, one] + thirds(norm + SPEED_FLOOR)
    p, q, t = weight, weight * radius, weight * radius * radius

    def halves(x):
        a = x.astype(BF16).astype(F32)
        return a, x - a

    (ph, pm), (qh, qm), (th, tm) = halves(p), halves(q), halves(t)
    left += [th, th, tm, 2.0 * qh, 2.0 * qh, 2.0 * qm, ph, ph, pm]
    right += [ph, pm, ph, qh, qm, qh, th, tm, th]
    return left, right


def cube_order(ids):
    column = columns_of(ids)
    ranks, counts = [], []
    for k in range(0, SLOTS, BLK):
        same = column == ids[:, k : k + BLK]
        earlier = iota((SLOTS, BLK), 0) < iota((SLOTS, BLK), 1) + k
        ranks.append(jnp.sum(jnp.where(earlier & same, 1.0, 0.0), axis=0, keepdims=True))
        counts.append(jnp.sum(jnp.where(same, 1.0, 0.0), axis=0, keepdims=True))
    rank, count = jnp.concatenate(ranks, axis=1), jnp.concatenate(counts, axis=1)
    key = (MOST - count) * 256.0 + ids
    first = (ids > 0.0) & (rank == 0.0)
    first_keys = columns_of(jnp.where(first, key, 1e9))
    before = [
        jnp.sum(jnp.where(first_keys < key[:, k : k + BLK], 1.0, 0.0), axis=0, keepdims=True)
        for k in range(0, SLOTS, BLK)
    ]
    place = jnp.where(ids > 0.0, jnp.concatenate(before, axis=1) * MOST + rank, -1.0)
    cubes = [
        jnp.broadcast_to(
            jnp.sum(jnp.where(first & (count >= n), 1, 0), axis=1, keepdims=True), (1, BLK)
        )
        for n in range(MOST, 0, -1)
    ]
    return place, jnp.concatenate(cubes + [jnp.zeros((4, BLK), jnp.int32)], axis=0)


def pair_kernel(next_in, grouped, counts, next_out, rate, left, right, moved, sem):
    next_load = pltpu.make_async_copy(next_in, moved, sem.at[0])
    next_load.start()
    lefts, rights = features([grouped[c] for c in range(5)])
    zero = jnp.zeros((SLOTS, BLK), F32)
    for f in range(KF):
        left[f * PITCH : f * PITCH + SLOTS, :] = lefts[f] if f < len(lefts) else zero
        right[f * PITCH : f * PITCH + SLOTS, :] = rights[f] if f < len(rights) else zero

    gap_rows = iota((KF, BLK), 0) < 18
    off_diag = iota((BLK, BLK), 0) != iota((BLK, BLK), 1)

    rate[...] = zero
    next_load.wait()
    next_copy = pltpu.make_async_copy(moved, next_out, sem.at[1])
    next_copy.start()

    def one_cube(q, members):
        base = q * MOST
        lhs = jnp.concatenate(
            [left[pl.ds(base + m, KF, stride=PITCH), :].astype(BF16) for m in range(members)], axis=1
        )
        row_sums = [None] * members
        out = []
        for c in range(members):
            r = right[pl.ds(base + c, KF, stride=PITCH), :]
            rhs = jnp.concatenate(
                [jnp.where(gap_rows, r, 0.0), jnp.where(gap_rows, 0.0, r)], axis=1
            ).astype(BF16)
            tiles = lax.dot_general(
                lhs[:, : (c + 1) * BLK], rhs, (((0,), (0,)), ((), ())), preferred_element_type=F32
            )
            total = None
            for a in range(c + 1):
                gap = jnp.maximum(tiles[a * BLK : (a + 1) * BLK, :BLK], SPEED_FLOOR)
                pair = tiles[a * BLK : (a + 1) * BLK, BLK:] * (gap * lax.rsqrt(gap))
                if a == c:
                    pair = jnp.where(off_diag, pair, 0.0)
                else:
                    row_sums[a] = pair if row_sums[a] is None else row_sums[a] + pair
                part = jnp.sum(pair.reshape(16, 8, BLK), axis=0)
                total = part if total is None else total + part
            out.append(total)
        for c in range(members):
            total = out[c]
            if row_sums[c] is not None:
                total = total + jnp.sum(jnp.transpose(row_sums[c]).reshape(16, 8, BLK), axis=0)
            rate[pl.ds(base + c, 1), :] = jnp.sum(total, axis=0, keepdims=True) * (1.0 / (MOST * BLK))

    done = 0
    for row, members in enumerate(range(MOST, 0, -1)):
        upto = lax.div(counts[row, 0] + (GROUP - 1), GROUP)

        def group(g, carry, members=members):
            for k in range(GROUP):
                one_cube(g * GROUP + k, members)
            return carry

        lax.fori_loop(done, upto, group, 0)
        done = upto

    next_copy.wait()


def return_kernel(
    sent, rate_in, place_in, slot_in, out, rate, place, slot, back, home, local_sem, send_sem, recv_sem
):
    me = lax.axis_index("space")
    place_copy = pltpu.make_async_copy(place_in, place, local_sem.at[0])
    rate_copy = pltpu.make_async_copy(rate_in, rate, local_sem.at[1])
    slot_copy = pltpu.make_async_copy(slot_in, slot, local_sem.at[2])
    place_copy.start()
    rate_copy.start()
    slot_copy.start()
    barrier = hello(me)
    place_copy.wait()
    rate_copy.wait()
    slot_copy.wait()
    back[...] = picked(one_hot_back(place[0:1, :]), rate[...]).reshape(NS, CAP, BLK)
    if sent < CAP:
        home[:, sent:, :] = jnp.zeros((NS, CAP - sent, BLK), F32)
    home[pl.ds(me, 1)] = back[pl.ds(me, 1)]
    pl.semaphore_wait(barrier, NS - 1)
    send_all(me, sent, back, home, send_sem, recv_sem)
    pick = one_hot_back(slot[0:1, :])
    wait_all(sent, home, recv_sem)
    out[...] = picked(pick, home[...].reshape(SLOTS, BLK))
    wait_all(sent, home, send_sem)


VMEM = pl.BlockSpec(memory_space=pltpu.VMEM)
ANY = pl.BlockSpec(memory_space=pl.ANY)
SMEM = pl.BlockSpec(memory_space=pltpu.SMEM)
LIMIT = 56 * 2**20
DMA = pltpu.SemaphoreType.DMA


def exchange_call(sent, orbit_state, object_props, table, cube):
    many = NB * BLK
    wide = pltpu.VMEM((NS, CAP if sent < CAP else CAP + 8, BLK), F32)
    return pl.pallas_call(
        functools.partial(exchange_kernel, sent),
        out_shape=(
            jax.ShapeDtypeStruct((6, many), F32),
            jax.ShapeDtypeStruct((5, SLOTS, BLK), F32),
            jax.ShapeDtypeStruct((8, SLOTS), F32),
            jax.ShapeDtypeStruct((8, BLK), jnp.int32),
            jax.ShapeDtypeStruct((8, NB), F32),
            jax.ShapeDtypeStruct((1, 1), jnp.int32),
        ),
        in_specs=[ANY, ANY, ANY, ANY],
        out_specs=(ANY, ANY, ANY, ANY, ANY, SMEM),
        scratch_shapes=[
            pltpu.VMEM((6, many), F32),
            pltpu.VMEM((3, many), F32),
            pltpu.VMEM((NB * 8, BLK), F32),
            pltpu.VMEM((NB * 8, BLK), F32),
            pltpu.VMEM((1, BLK), F32),
            pltpu.VMEM((NS, 1, BLK), F32),
            pltpu.VMEM((NS, CAP, BLK), F32),
            wide,
            pltpu.VMEM((3, NS, CAP, BLK), F32),
            pltpu.VMEM((NS, CAP, BLK), F32),
            wide,
            pltpu.VMEM((3, NS, CAP, BLK), F32),
            pltpu.VMEM((5, SLOTS, BLK), F32),
            pltpu.VMEM((8, NB), F32),
            pltpu.VMEM((8, SLOTS), F32),
            pltpu.VMEM((8, BLK), jnp.int32),
            pltpu.VMEM((1, NTAB), F32),
            pltpu.VMEM((1, NB), jnp.int32),
            DMA((7,)),
            DMA((5,)),
            DMA,
            DMA,
            DMA((5,)),
            DMA((5,)),
        ],
        compiler_params=pltpu.CompilerParams(
            collective_id=0 if sent < CAP else 2, has_side_effects=True, vmem_limit_bytes=LIMIT
        ),
        name="exchange",
    )(orbit_state, object_props, table, cube)


def pair_call(next_state, grouped, counts):
    return pl.pallas_call(
        pair_kernel,
        out_shape=(
            jax.ShapeDtypeStruct(next_state.shape, F32),
            jax.ShapeDtypeStruct((SLOTS, BLK), F32),
        ),
        in_specs=[ANY, VMEM, SMEM],
        out_specs=(ANY, VMEM),
        scratch_shapes=[
            pltpu.VMEM((KF * PITCH, BLK), F32),
            pltpu.VMEM((KF * PITCH, BLK), F32),
            pltpu.VMEM(next_state.shape, F32),
            DMA((2,)),
        ],
        compiler_params=pltpu.CompilerParams(vmem_limit_bytes=LIMIT),
        name="pairs",
    )(next_state, grouped, counts)


def return_call(sent, rate, place, slot):
    return pl.pallas_call(
        functools.partial(return_kernel, sent),
        out_shape=jax.ShapeDtypeStruct((NB, BLK), F32),
        in_specs=[ANY, ANY, ANY],
        out_specs=VMEM,
        scratch_shapes=[
            pltpu.VMEM((SLOTS, BLK), F32),
            pltpu.VMEM((8, SLOTS), F32),
            pltpu.VMEM((8, NB), F32),
            pltpu.VMEM((NS, CAP, BLK), F32),
            pltpu.VMEM((NS, CAP, BLK), F32),
            DMA((3,)),
            DMA,
            DMA,
        ],
        compiler_params=pltpu.CompilerParams(
            collective_id=1 if sent < CAP else 3, has_side_effects=True, vmem_limit_bytes=LIMIT
        ),
        name="bring_home",
    )(rate, place, slot)


def on_device(orbit_state, object_props, density_table, block_cube):
    args = (orbit_state, object_props, density_table.reshape(1, 64), block_cube.reshape(1, NB))

    def attempt(sent):
        moved, grouped, place, counts, slot, found = exchange_call(sent, *args)
        next_state, rate = pair_call(moved, grouped, counts)
        return next_state, return_call(sent, rate, place, slot), found.reshape(())

    def again(carry):
        return (attempt(CAP)[1], jnp.int32(1))

    next_state, rate, found = attempt(SENT)
    rate, _ = lax.while_loop(lambda carry: carry[1] == 0, again, (rate, found))
    return next_state, rate.reshape(NB * BLK)


def solution(mesh):
    placed = (P(None, ("mc", "space")), P(None, ("mc", "space")), P(), P(("mc", "space")))
    return jax.shard_map(
        on_device,
        mesh=mesh,
        in_specs=placed,
        out_specs=(P(None, ("mc", "space")), P(("mc", "space"))),
        check_vma=False,
    )
```

```python
import functools

import jax
import jax.numpy as jnp
from jax import lax
from jax.experimental import pallas as pl
from jax.experimental.pallas import tpu as pltpu
from jax.sharding import PartitionSpec as P

F32 = jnp.float32
BF16 = jnp.bfloat16
MESH = pl.DeviceIdType.MESH
BLK = 128
NB = 256
NS = 16
CAP = 32
SENT = 25
SLOTS = NS * CAP
CUBES = 128
MOST = 4
NTAB = 64
SUB = 16
EARLY = 8
GROUPS = (8, 16, 16, 32)
SPARE = MOST * 32
KF = 32
PITCH = SLOTS + SPARE + 8

TIME_STEP = 0.2
EARTH_SPIN = 0.0588
J2_COEF = 0.00108263
DRAG_SCALE = 0.008
TABLE_SCALE = 63 / 0.4
SPEED_FLOOR = 0.04


def iota(shape, dim):
    return lax.broadcasted_iota(jnp.int32, shape, dim)


def split2(x):
    high = x.astype(BF16)
    return high, (x - high.astype(F32)).astype(BF16)


def columns_of(row):
    parts = [
        jnp.transpose(jnp.broadcast_to(row[:, k : k + BLK], (BLK, BLK)))
        for k in range(0, row.shape[1], BLK)
    ]
    return jnp.concatenate(parts, axis=0)


def rank_row(row):
    n = row.shape[1]
    column = columns_of(row)
    ranks = []
    for k in range(0, n, BLK):
        earlier = iota((n, BLK), 0) < iota((n, BLK), 1) + k
        same = column == row[:, k : k + BLK]
        ranks.append(jnp.sum(jnp.where(earlier & same, 1.0, 0.0), axis=0, keepdims=True))
    return jnp.concatenate(ranks, axis=1)


def balanced(cube, k):
    high = lax.shift_right_logical(cube, 4)
    return ((cube & 15) + lax.shift_right_logical(high * (37 * k + 11), 4)) & 15


def substep(x, y, z, vx, vy, vz, drag, tab, slope):
    r2 = x * x + y * y + z * z
    ri = lax.rsqrt(r2)
    h = r2 * ri - 1.0
    coord = jnp.clip(h * TABLE_SCALE, -1.0, 64.0)
    below = jnp.floor(coord)
    frac = coord - below
    index = below.astype(jnp.int32) + 1
    base = jnp.concatenate(
        [jnp.take_along_axis(tab, index[k : k + 8], axis=1) for k in range(0, x.shape[0], 8)], axis=0
    )
    rise = jnp.concatenate(
        [jnp.take_along_axis(slope, index[k : k + 8], axis=1) for k in range(0, x.shape[0], 8)], axis=0
    )
    density = jnp.exp(base + frac * rise - h * 10.0)
    ux = vx + EARTH_SPIN * y
    uy = vy - EARTH_SPIN * x
    u2 = ux * ux + uy * uy + vz * vz
    speed = u2 * lax.rsqrt(jnp.maximum(u2, 1e-36))
    pull = density * drag * speed
    i2 = ri * ri
    i3 = i2 * ri
    oblate = (1.5 * J2_COEF * TIME_STEP) * (i2 * i3)
    near = TIME_STEP * i3 + oblate * (1.0 - 5.0 * (z * z * i2))
    vx = vx - x * near - pull * ux
    vy = vy - y * near - pull * uy
    vz = vz - z * (near + 2.0 * oblate) - pull * vz
    return x + TIME_STEP * vx, y + TIME_STEP * vy, z + TIME_STEP * vz, vx, vy, vz


def hello(me):
    barrier = pltpu.get_barrier_semaphore()
    for k in range(1, NS):
        pl.semaphore_signal(
            barrier, inc=1, device_id={"space": (me + k) & (NS - 1)}, device_id_type=MESH
        )
    return barrier


def send_all(me, count, out_of, into, send_sem, recv_sem):
    for k in range(1, NS):
        to = (me + k) & (NS - 1)
        pltpu.make_async_remote_copy(
            src_ref=out_of.at[to, pl.ds(0, count)],
            dst_ref=into.at[me, pl.ds(0, count)],
            send_sem=send_sem,
            recv_sem=recv_sem,
            device_id={"space": to},
            device_id_type=MESH,
        ).start()


def wait_all(count, into, sem):
    others = into.at[pl.ds(0, NS - 1), pl.ds(0, count)]
    pltpu.make_async_copy(others, others, sem).wait()


def one_hot(place, n):
    width = place.shape[1]
    return jnp.where(place == iota((n, width), 0).astype(F32), 1.0, 0.0).astype(BF16)


def one_hot_back(place):
    column = columns_of(place)
    n = place.shape[1]
    parts = [
        jnp.where(column == (iota((n, BLK), 1) + k).astype(F32), 1.0, 0.0)
        for k in range(0, SLOTS, BLK)
    ]
    return jnp.concatenate(parts, axis=1).astype(BF16)


def picked(pick, plane):
    high, low = split2(plane)
    got = jnp.dot(pick, jnp.concatenate([high, low], axis=1), preferred_element_type=F32)
    return got[:, :BLK] + got[:, BLK:]


def exchange_kernel(
    sent, orbit_in, props_in, table_in, cube_in, next_out, grouped_out, place_out, count_out, slot_out, found_out,
    orbit, props, rows, prows, need, needs, send_r, send_w, send_b, recv_r, recv_w, recv_b, grouped,
    slot_at, place_at, count_at, table, cube, local_sem, group_sem, need_send, need_recv, sends, recvs,
):
    me = lax.axis_index("space")
    cube_copy = pltpu.make_async_copy(cube_in, cube, local_sem.at[5])
    table_copy = pltpu.make_async_copy(table_in, table, local_sem.at[6])
    cube_copy.start()
    barrier = hello(me)
    table_copy.start()
    orbit_copy = pltpu.make_async_copy(orbit_in, orbit, local_sem.at[0])
    props_copy = pltpu.make_async_copy(props_in, props, local_sem.at[1])
    props_copy.start()
    orbit_copy.start()
    cube_copy.wait()

    if sent < CAP:
        column = columns_of(cube[...].astype(F32)).astype(jnp.int32)
        to = balanced(column, iota((NB, BLK), 1))
        most = jnp.zeros((1, BLK), F32)
        for device in range(NS):
            held = jnp.sum(jnp.where(to == device, 1.0, 0.0), axis=0, keepdims=True)
            most = jnp.maximum(most, held)
        need[...] = most
        needs[pl.ds(me, 1)] = need[...][None]
        pl.semaphore_wait(barrier, NS - 1)
        for k in range(1, NS):
            pltpu.make_async_remote_copy(
                src_ref=need,
                dst_ref=needs.at[me],
                send_sem=need_send,
                recv_sem=need_recv,
                device_id={"space": (me + k) & (NS - 1)},
                device_id_type=MESH,
            ).start()
        recv_r[:, sent:, :] = jnp.zeros((NS, CAP - sent, BLK), F32)
        recv_w[:, sent + 1 :, :] = jnp.zeros((NS, CAP - sent - 1, BLK), F32)
        for c in range(3):
            recv_b[c, :, sent:, :] = jnp.zeros((NS, CAP - sent, BLK), F32)
    else:
        pl.semaphore_wait(barrier, NS - 1)

    table_copy.wait()
    props_copy.wait()
    orbit_copy.wait()

    def spread(b, carry):
        col = pl.ds(pl.multiple_of(b * BLK, BLK), BLK)
        at = pl.multiple_of(b * 8, 8)
        rows[pl.ds(at, 6), :] = orbit[:, col]
        prows[pl.ds(at, 3), :] = props[:, col]
        return carry

    lax.fori_loop(0, NB, spread, 0, unroll=8)

    def load(ref, c):
        return jnp.concatenate(
            [ref[pl.ds(k * 8 + c, 8, stride=8), :] for k in range(0, NB, 8)], axis=0
        )

    tab = jnp.concatenate([table[...], jnp.zeros((1, 64), F32)], axis=1)
    tab = pltpu.roll(jnp.broadcast_to(tab, (8, BLK)), 1, 1)
    slope = pltpu.roll(tab, BLK - 1, 1) - tab
    now = tuple(load(rows, c) for c in range(6))
    drag = load(prows, 2) * (DRAG_SCALE * TIME_STEP)
    advance = lambda s, v: substep(*v, drag, tab, slope)
    now = lax.fori_loop(0, EARLY, advance, now, unroll=4)
    if sent < CAP:
        wait_all(1, needs, need_recv)
        fits = jnp.max(needs[...], axis=0) <= sent
        lane = iota((1, BLK), 1).astype(F32)
        first = jnp.min(jnp.where(fits, lane, float(BLK)), axis=1, keepdims=True)
        found = first < BLK
        to = balanced(cube[...], jnp.where(found, first, 0.0).astype(jnp.int32))
        local = lax.shift_right_logical(cube[...], 4)
    else:
        found = None
        to = lax.shift_right_logical(cube[...], 7)
        local = cube[...] & (CUBES - 1)
    slot = to.astype(F32) * CAP + rank_row(to.astype(F32))
    slot_at[...] = jnp.broadcast_to(slot, (8, NB))
    slot_copy = pltpu.make_async_copy(slot_at, slot_out, local_sem.at[2])
    slot_copy.start()
    pick = one_hot(slot, SLOTS)
    send_r[...] = picked(pick, load(prows, 0)).reshape(NS, CAP, BLK)
    send_all(me, sent, send_r, recv_r, sends.at[3], recvs.at[3])
    send_w[:, :CAP, :] = picked(pick, load(prows, 1)).reshape(NS, CAP, BLK)
    ids = jnp.dot(
        pick, columns_of((local + 1).astype(F32)).astype(BF16), preferred_element_type=F32
    )
    id_rows = []
    for q in range(SLOTS // BLK):
        line = jnp.transpose(ids[q * BLK : (q + 1) * BLK])[0:1]
        id_rows.append(jnp.broadcast_to(line, (4, BLK)))
    id_rows = jnp.concatenate(id_rows, axis=0)
    mine = lax.shift_right_logical(iota((NS, BLK), 1), 5) == (iota((NS, BLK), 0) & 3)
    id_rows = jnp.where(mine, id_rows, 0.0)
    id_rows = id_rows + pltpu.roll(id_rows, 64, 1)
    id_rows = id_rows + pltpu.roll(id_rows, 32, 1)
    send_w[:, sent : sent + 1, :] = id_rows[:, None, :]
    send_all(me, sent + 1, send_w, recv_w, sends.at[4], recvs.at[4])
    recv_w[pl.ds(me, 1)] = send_w[pl.ds(me, 1)]
    recv_r[pl.ds(me, 1)] = send_r[pl.ds(me, 1)]

    now = lax.fori_loop(EARLY, SUB, advance, now, unroll=4)
    for c in range(6):
        for k in range(0, NB, 8):
            rows[pl.ds(k * 8 + c, 8, stride=8), :] = now[c][k : k + 8]
    for c in range(3):
        send_b[c] = picked(pick, load(rows, 3 + c)).reshape(NS, CAP, BLK)
        send_all(me, sent, send_b.at[c], recv_b.at[c], sends.at[c], recvs.at[c])

    def collect(b, carry):
        col = pl.ds(pl.multiple_of(b * BLK, BLK), BLK)
        orbit[:, col] = rows[pl.ds(pl.multiple_of(b * 8, 8), 6), :]
        return carry

    lax.fori_loop(0, NB, collect, 0, unroll=8)
    next_copy = pltpu.make_async_copy(orbit, next_out, local_sem.at[0])
    next_copy.start()
    for c in range(3):
        recv_b[c, pl.ds(me, 1)] = send_b[c, pl.ds(me, 1)]

    wait_all(sent + 1, recv_w, recvs.at[4])
    got = jnp.where(mine, recv_w[:, sent, :], 0.0)
    ids = jnp.concatenate(
        [jnp.sum(got[4 * q : 4 * q + 4], axis=0, keepdims=True) for q in range(4)], axis=1
    )
    place, counts = cube_order(ids)
    place_at[...] = jnp.broadcast_to(place, (8, SLOTS))
    place_copy = pltpu.make_async_copy(place_at, place_out, local_sem.at[3])
    place_copy.start()
    if found is None:
        count_at[...] = counts
        found_out[0, 0] = jnp.int32(1)
    else:
        found_out[0, 0] = jnp.where(found, 1, 0)[0, 0]
        count_at[...] = jnp.where(found, jnp.minimum(counts, CUBES), 0)
    count_copy = pltpu.make_async_copy(count_at, count_out, local_sem.at[4])
    count_copy.start()
    pick = one_hot(place, SLOTS)

    def regroup(c, plane):
        grouped[c] = picked(pick, plane.reshape(SLOTS, BLK))
        copy = pltpu.make_async_copy(grouped.at[c], grouped_out.at[c], group_sem.at[c])
        copy.start()
        return copy

    copies = [regroup(4, recv_w[:, :CAP, :])]
    wait_all(sent, recv_r, recvs.at[3])
    copies.append(regroup(3, recv_r[...]))
    for c in range(3):
        wait_all(sent, recv_b.at[c], recvs.at[c])
        copies.append(regroup(c, recv_b[c]))
    if sent < CAP:
        wait_all(1, needs, need_send)
    wait_all(sent + 1, recv_w, sends.at[4])
    wait_all(sent, recv_r, sends.at[3])
    for c in range(3):
        wait_all(sent, recv_b.at[c], sends.at[c])
    for copy in copies:
        copy.wait()
    for copy in (slot_copy, place_copy, count_copy, next_copy):
        copy.wait()


def features(planes):
    radius, weight = planes[3], planes[4]
    v = []
    for full in planes[:3]:
        high = full.astype(BF16).astype(F32)
        v.append((high, full - high))
    norm = planes[0] * planes[0] + planes[1] * planes[1] + planes[2] * planes[2]

    def thirds(x):
        a = x.astype(BF16).astype(F32)
        b = (x - a).astype(BF16).astype(F32)
        return [a, b, x - a - b]

    one = jnp.ones_like(radius)
    left, right = [], []
    for h, m in v:
        left += [h, h, m, m]
        right += [-2.0 * h, -2.0 * m, -2.0 * h, -2.0 * m]
    left += thirds(norm) + [one, one, one]
    right += [one, one, one] + thirds(norm + SPEED_FLOOR)
    p, q, t = weight, weight * radius, weight * radius * radius

    def halves(x):
        a = x.astype(BF16).astype(F32)
        return a, x - a

    (ph, pm), (qh, qm), (th, tm) = halves(p), halves(q), halves(t)
    left += [th, th, tm, 2.0 * qh, 2.0 * qh, 2.0 * qm, ph, ph, pm]
    right += [ph, pm, ph, qh, qm, qh, th, tm, th]
    return left, right


def cube_order(ids):
    column = columns_of(ids)
    ranks, counts = [], []
    for k in range(0, SLOTS, BLK):
        same = column == ids[:, k : k + BLK]
        earlier = iota((SLOTS, BLK), 0) < iota((SLOTS, BLK), 1) + k
        ranks.append(jnp.sum(jnp.where(earlier & same, 1.0, 0.0), axis=0, keepdims=True))
        counts.append(jnp.sum(jnp.where(same, 1.0, 0.0), axis=0, keepdims=True))
    rank, count = jnp.concatenate(ranks, axis=1), jnp.concatenate(counts, axis=1)
    key = (MOST - count) * 256.0 + ids
    first = (ids > 0.0) & (rank == 0.0)
    first_keys = columns_of(jnp.where(first, key, 1e9))
    before = [
        jnp.sum(jnp.where(first_keys < key[:, k : k + BLK], 1.0, 0.0), axis=0, keepdims=True)
        for k in range(0, SLOTS, BLK)
    ]
    place = jnp.where(ids > 0.0, jnp.concatenate(before, axis=1) * MOST + rank, -1.0)
    cubes = [
        jnp.broadcast_to(
            jnp.sum(jnp.where(first & (count >= n), 1, 0), axis=1, keepdims=True), (1, BLK)
        )
        for n in range(MOST, 0, -1)
    ]
    return place, jnp.concatenate(cubes + [jnp.zeros((4, BLK), jnp.int32)], axis=0)


def pair_kernel(next_in, grouped, counts, next_out, rate, left, right, moved, sem):
    next_load = pltpu.make_async_copy(next_in, moved, sem.at[0])
    next_load.start()
    lefts, rights = features([grouped[c] for c in range(5)])
    zero = jnp.zeros((SLOTS, BLK), F32)
    for f in range(KF):
        left[f * PITCH : f * PITCH + SLOTS, :] = lefts[f] if f < len(lefts) else zero
        right[f * PITCH : f * PITCH + SLOTS, :] = rights[f] if f < len(rights) else zero

    gap_rows = iota((KF, BLK), 0) < 18
    off_diag = iota((BLK, BLK), 0) != iota((BLK, BLK), 1)

    rate[:SLOTS, :] = zero
    next_load.wait()
    next_copy = pltpu.make_async_copy(moved, next_out, sem.at[1])
    next_copy.start()

    def one_cube(q, members):
        base = q * MOST
        lhs = jnp.concatenate(
            [left[pl.ds(base + m, KF, stride=PITCH), :].astype(BF16) for m in range(members)], axis=1
        )
        row_sums = [None] * members
        out = []
        for c in range(members):
            r = right[pl.ds(base + c, KF, stride=PITCH), :]
            rhs = jnp.concatenate(
                [jnp.where(gap_rows, r, 0.0), jnp.where(gap_rows, 0.0, r)], axis=1
            ).astype(BF16)
            tiles = lax.dot_general(
                lhs[:, : (c + 1) * BLK], rhs, (((0,), (0,)), ((), ())), preferred_element_type=F32
            )
            total = None
            for a in range(c + 1):
                gap = jnp.maximum(tiles[a * BLK : (a + 1) * BLK, :BLK], SPEED_FLOOR)
                pair = tiles[a * BLK : (a + 1) * BLK, BLK:] * (gap * lax.rsqrt(gap))
                if a == c:
                    pair = jnp.where(off_diag, pair, 0.0)
                else:
                    row_sums[a] = pair if row_sums[a] is None else row_sums[a] + pair
                part = jnp.sum(pair.reshape(16, 8, BLK), axis=0)
                total = part if total is None else total + part
            out.append(total)
        for c in range(members):
            total = out[c]
            if row_sums[c] is not None:
                total = total + jnp.sum(jnp.transpose(row_sums[c]).reshape(16, 8, BLK), axis=0)
            rate[pl.ds(base + c, 1), :] = jnp.sum(total, axis=0, keepdims=True) * (1.0 / (MOST * BLK))

    done = 0
    for row, size in enumerate(GROUPS):
        steps = lax.div(jnp.maximum(counts[row, 0] - done, 0) + (size - 1), size)

        def group(g, carry, first=done, size=size, members=MOST - row):
            for k in range(size):
                one_cube(first + g * size + k, members)
            return carry

        lax.fori_loop(0, steps, group, 0)
        done = done + steps * size

    next_copy.wait()


def return_kernel(
    sent, rate_in, place_in, slot_in, out, rate, place, slot, back, home, local_sem, send_sem, recv_sem
):
    me = lax.axis_index("space")
    place_copy = pltpu.make_async_copy(place_in, place, local_sem.at[0])
    rate_copy = pltpu.make_async_copy(rate_in, rate, local_sem.at[1])
    slot_copy = pltpu.make_async_copy(slot_in, slot, local_sem.at[2])
    place_copy.start()
    rate_copy.start()
    slot_copy.start()
    barrier = hello(me)
    place_copy.wait()
    rate_copy.wait()
    slot_copy.wait()
    back[...] = picked(one_hot_back(place[0:1, :]), rate[:SLOTS, :]).reshape(NS, CAP, BLK)
    if sent < CAP:
        home[:, sent:, :] = jnp.zeros((NS, CAP - sent, BLK), F32)
    home[pl.ds(me, 1)] = back[pl.ds(me, 1)]
    pl.semaphore_wait(barrier, NS - 1)
    send_all(me, sent, back, home, send_sem, recv_sem)
    pick = one_hot_back(slot[0:1, :])
    wait_all(sent, home, recv_sem)
    out[...] = picked(pick, home[...].reshape(SLOTS, BLK))
    wait_all(sent, home, send_sem)


VMEM = pl.BlockSpec(memory_space=pltpu.VMEM)
ANY = pl.BlockSpec(memory_space=pl.ANY)
SMEM = pl.BlockSpec(memory_space=pltpu.SMEM)
LIMIT = 56 * 2**20
DMA = pltpu.SemaphoreType.DMA


def exchange_call(sent, orbit_state, object_props, table, cube):
    many = NB * BLK
    wide = pltpu.VMEM((NS, CAP if sent < CAP else CAP + 8, BLK), F32)
    return pl.pallas_call(
        functools.partial(exchange_kernel, sent),
        out_shape=(
            jax.ShapeDtypeStruct((6, many), F32),
            jax.ShapeDtypeStruct((5, SLOTS, BLK), F32),
            jax.ShapeDtypeStruct((8, SLOTS), F32),
            jax.ShapeDtypeStruct((8, BLK), jnp.int32),
            jax.ShapeDtypeStruct((8, NB), F32),
            jax.ShapeDtypeStruct((1, 1), jnp.int32),
        ),
        in_specs=[ANY, ANY, ANY, ANY],
        out_specs=(ANY, ANY, ANY, ANY, ANY, SMEM),
        scratch_shapes=[
            pltpu.VMEM((6, many), F32),
            pltpu.VMEM((3, many), F32),
            pltpu.VMEM((NB * 8, BLK), F32),
            pltpu.VMEM((NB * 8, BLK), F32),
            pltpu.VMEM((1, BLK), F32),
            pltpu.VMEM((NS, 1, BLK), F32),
            pltpu.VMEM((NS, CAP, BLK), F32),
            wide,
            pltpu.VMEM((3, NS, CAP, BLK), F32),
            pltpu.VMEM((NS, CAP, BLK), F32),
            wide,
            pltpu.VMEM((3, NS, CAP, BLK), F32),
            pltpu.VMEM((5, SLOTS, BLK), F32),
            pltpu.VMEM((8, NB), F32),
            pltpu.VMEM((8, SLOTS), F32),
            pltpu.VMEM((8, BLK), jnp.int32),
            pltpu.VMEM((1, NTAB), F32),
            pltpu.VMEM((1, NB), jnp.int32),
            DMA((7,)),
            DMA((5,)),
            DMA,
            DMA,
            DMA((5,)),
            DMA((5,)),
        ],
        compiler_params=pltpu.CompilerParams(
            collective_id=0 if sent < CAP else 2, has_side_effects=True, vmem_limit_bytes=LIMIT
        ),
        name="exchange",
    )(orbit_state, object_props, table, cube)


def pair_call(next_state, grouped, counts):
    return pl.pallas_call(
        pair_kernel,
        out_shape=(
            jax.ShapeDtypeStruct(next_state.shape, F32),
            jax.ShapeDtypeStruct((SLOTS + SPARE, BLK), F32),
        ),
        in_specs=[ANY, VMEM, SMEM],
        out_specs=(ANY, VMEM),
        scratch_shapes=[
            pltpu.VMEM((KF * PITCH, BLK), F32),
            pltpu.VMEM((KF * PITCH, BLK), F32),
            pltpu.VMEM(next_state.shape, F32),
            DMA((2,)),
        ],
        compiler_params=pltpu.CompilerParams(vmem_limit_bytes=LIMIT),
        name="pairs",
    )(next_state, grouped, counts)


def return_call(sent, rate, place, slot):
    return pl.pallas_call(
        functools.partial(return_kernel, sent),
        out_shape=jax.ShapeDtypeStruct((NB, BLK), F32),
        in_specs=[ANY, ANY, ANY],
        out_specs=VMEM,
        scratch_shapes=[
            pltpu.VMEM((SLOTS + SPARE, BLK), F32),
            pltpu.VMEM((8, SLOTS), F32),
            pltpu.VMEM((8, NB), F32),
            pltpu.VMEM((NS, CAP, BLK), F32),
            pltpu.VMEM((NS, CAP, BLK), F32),
            DMA((3,)),
            DMA,
            DMA,
        ],
        compiler_params=pltpu.CompilerParams(
            collective_id=1 if sent < CAP else 3, has_side_effects=True, vmem_limit_bytes=LIMIT
        ),
        name="bring_home",
    )(rate, place, slot)


def on_device(orbit_state, object_props, density_table, block_cube):
    args = (orbit_state, object_props, density_table.reshape(1, 64), block_cube.reshape(1, NB))

    def attempt(sent):
        moved, grouped, place, counts, slot, found = exchange_call(sent, *args)
        next_state, rate = pair_call(moved, grouped, counts)
        return next_state, return_call(sent, rate, place, slot), found.reshape(())

    def again(carry):
        return (attempt(CAP)[1], jnp.int32(1))

    next_state, rate, found = attempt(SENT)
    rate, _ = lax.while_loop(lambda carry: carry[1] == 0, again, (rate, found))
    return next_state, rate.reshape(NB * BLK)


def solution(mesh):
    placed = (P(None, ("mc", "space")), P(None, ("mc", "space")), P(), P(("mc", "space")))
    return jax.shard_map(
        on_device,
        mesh=mesh,
        in_specs=placed,
        out_specs=(P(None, ("mc", "space")), P(("mc", "space"))),
        check_vma=False,
    )
```
